256 devices in a mesh: dp: 32 (over z, y), mp: 8 (over x, core).
Axes of the slice: x: 4, y: 4, z: 8, core: 2. Of those that a mesh axis runs over, the one named last changes fastest.
Arguments:
- activations: bfloat16 [8192, 8192], P('dp'), may hold values from -6 to 6
- cotangents: bfloat16 [2, 8192, 1024], P(None, 'dp', 'mp'), may hold values from -0.0625 to 0.0625
- worker_of: int32 [32], replicated, may hold values from 0 to 31, as said below
- left_stats: float32 [32, 2, 512, 512], P('dp'), as said below
Outputs:
- new_stats: float32 [32, 2, 512, 512], P('dp')
- roots: float32 [32, 2, 512, 512], P('dp')
- update: bfloat16 [32, 512, 1024], P('dp', None, 'mp')
The draws below stay inside these ranges and needn't reach their ends.
Inputs may be any that keep to these rules, and one draw needn't show every extreme that they name: `worker_of`: no worker is named by more than 2 blocks; some worker is named by exactly 2: the blocks k * 2 to k * 2 + 1 for some k. `left_stats`: every slot holds a symmetric positive definite matrix; slots that no block occupies are ignored.
All inputs are finite; a program needn't handle non-finite values.
Results may differ from the reference program's by a relative error of at most 0.005.
Values may be sent and summed in bfloat16 or wider, within the bound.
No kernel may reach another device: no remote copies, remote signals or barrier semaphores. Data moves between devices by JAX's collectives and lax.ppermute only.
A program may use at most 128 MiB of HBM per device.

```python
import math
import jax
import jax.numpy as jnp
from jax import lax

D = 8192
KV = 1024
BLOCK = 512
ITERS = 3
TOKENS = 8192
NB = 32
MOST = 2
N_DP = 32


def draw_worker_of(key, part):
    key = jax.random.fold_in(key, 11)
    key_pair = jax.random.fold_in(key, 0)
    key_scores = jax.random.fold_in(key, 2)
    pair_index = jax.random.randint(key_pair, (), 0, N_DP // 2)
    owner_first = pair_index * MOST // (NB // N_DP)
    chosen = (owner_first + N_DP // 2) % N_DP
    block_index = jnp.arange(NB, dtype=jnp.int32)
    crowded = block_index // MOST == pair_index
    slot_total = N_DP * MOST
    slot_range = jnp.arange(slot_total, dtype=jnp.int32)
    scores = jax.random.randint(key_scores, (slot_total,), 0, 1 << 20) * slot_total + slot_range
    scores = jnp.where(slot_range // MOST == chosen, (1 << 30) + slot_range, scores)
    ranking = jnp.argsort(scores)
    position = jnp.cumsum(1 - crowded.astype(jnp.int32)) - 1
    picked = ranking[jnp.clip(position, 0, slot_total - 1)] // MOST
    return jnp.where(crowded, chosen, picked).astype(jnp.int32)


def draw_left_stats(key, part):
    key = jax.random.fold_in(key, 23)
    key_points, key_boost, key_scale = jax.random.split(key, 3)
    spread = math.log(10.0)
    reach = 4.0
    points = BLOCK * jax.random.uniform(key_points, (N_DP, MOST, BLOCK), jnp.float32)
    distance = jnp.abs(points[..., :, None] - points[..., None, :])
    kernel = jnp.exp(-distance / reach)
    identity = jnp.eye(BLOCK, dtype=jnp.float32)
    boost = jax.random.uniform(key_boost, (N_DP, MOST, BLOCK), jnp.float32, 1.0, 2.0)
    core = kernel + identity * (0.5 * boost)[..., None]
    scales = jnp.exp(0.5 * spread * jax.random.uniform(key_scale, (N_DP, MOST, BLOCK), jnp.float32))
    return core * scales[..., :, None] * scales[..., None, :]


def block_scale(rng, dims, cuts, least, largest):
    gain = 1.0
    for dim, shards_of in cuts:
        draws = jax.random.uniform(jax.random.fold_in(jax.random.fold_in(rng, 6), dim), (shards_of,), jnp.float32, least / len(cuts), largest / len(cuts))
        gain = gain * jnp.repeat(jnp.exp(draws), dims[dim] // shards_of).reshape((-1,) + (1,) * (len(dims) - 1 - dim))
    return gain


def scatter_about(key, shape, scale, limit, cuts=(), held_as=jnp.bfloat16):
    drawn = jax.random.normal(key, shape, jnp.float32) * scale
    if len(cuts) > 0:
        drawn = block_scale(key, shape, cuts, -0.22, 0.18) * drawn
    return jnp.clip(drawn, min=-limit, max=limit).astype(held_as)


def setup_inputs(seed: int = 0) -> dict:
    splits = jax.random.split(jax.random.key(seed), 5)
    return {
        "activations": scatter_about(splits[0], (TOKENS, D), 1.0, 6.0, ((0, 32),)),
        "cotangents": scatter_about(splits[1], (2, TOKENS, KV), TOKENS ** -0.5, 0.0625, ((1, 32), (2, 8))),
        "worker_of": draw_worker_of(jax.random.fold_in(splits[4], 71), 0),
        "left_stats": draw_left_stats(jax.random.fold_in(splits[4], 71), 0),
    }


def product(left, right):
    return jnp.dot(left, right, precision=lax.Precision.HIGHEST)

def fourth_root(matrix):
    dimension = matrix.shape[-1]
    identity = jnp.eye(dimension, dtype=jnp.float32)
    norm_value = jnp.sqrt(jnp.sum(matrix * matrix))
    root_mat = identity * norm_value ** (-0.25)
    power = matrix / norm_value
    for iteration in range(ITERS):
        factor = (5.0 * identity - power) * 0.25
        root_mat = product(root_mat, factor)
        square = product(factor, factor)
        power = product(product(square, square), power)
    return root_mat

def reference(activations, cotangents, worker_of, left_stats):
    per_matrix = D // BLOCK
    inputs_wide = activations.astype(jnp.float32)
    pieces = []
    for projection in range(2):
        whole_grad = jnp.dot(inputs_wide.T, cotangents[projection].astype(jnp.float32), precision=lax.Precision.HIGHEST)
        pieces.append(whole_grad.reshape(per_matrix, BLOCK, KV))
    grad_blocks = jnp.concatenate(pieces, axis=0).astype(jnp.bfloat16)
    block_index = jnp.arange(NB, dtype=jnp.int32)
    earlier = (worker_of[None, :] == worker_of[:, None]) & (block_index[None, :] < block_index[:, None])
    slot_of = lax.optimization_barrier(jnp.sum(earlier.astype(jnp.int32), axis=1)).astype(jnp.int32)
    slot_key = (worker_of * MOST + slot_of).astype(jnp.int32)
    flat_stats = left_stats.reshape(N_DP * MOST, BLOCK, BLOCK)
    slot_range = jnp.arange(N_DP * MOST, dtype=jnp.int32)
    occupied = jnp.any(slot_key[None, :] == slot_range[:, None], axis=1).astype(jnp.float32)
    newton_root = lax.map(fourth_root, flat_stats)
    root_mats = newton_root * occupied[:, None, None]
    grad_wide = grad_blocks.astype(jnp.float32)
    gram_total = jnp.einsum('nbk,nck->nbc', grad_wide, grad_wide, precision=lax.Precision.HIGHEST) * (1.0 / KV)
    new_stats = jnp.zeros_like(flat_stats).at[slot_key].set(flat_stats[slot_key] + gram_total)
    update = jnp.einsum('nbc,nck->nbk', root_mats[slot_key], grad_wide, precision=lax.Precision.HIGHEST)
    return (new_stats.reshape(N_DP, MOST, BLOCK, BLOCK), root_mats.reshape(N_DP, MOST, BLOCK, BLOCK), update.astype(jnp.bfloat16))
```

```python
import jax
import jax.numpy as jnp
from jax import lax
from jax.sharding import Mesh, PartitionSpec as P

KV = 1024
NZ, NY, NX, NC = 8, 4, 4, 2
BF = jnp.bfloat16
F32 = jnp.float32


def shift(x, axis, size, offset):
    return lax.ppermute(x, axis, [(i, (i + offset) % size) for i in range(size)])


def pick(parts, index):
    return lax.dynamic_index_in_dim(parts, index, 0, keepdims=False)


def batch_product(left, right):
    return jnp.einsum("sij,sjk->sik", left, right, precision=lax.Precision.HIGH, preferred_element_type=F32)


def fourth_roots(matrices):
    identity = jnp.eye(matrices.shape[-1], dtype=F32)[None]
    norm_values = jnp.sqrt(jnp.sum(matrices * matrices, axis=(1, 2)))[:, None, None]
    m = matrices / norm_values
    m2 = batch_product(m, m)
    z = (5.0 * identity - m) * 0.25
    z2 = (25.0 * identity - 10.0 * m + m2) * (1.0 / 16.0)
    u = (5.0 * m - m2) * 0.25
    z4 = batch_product(z2, z2)
    x1 = 1.25 * z - 0.25 * batch_product(z4, u)
    s = batch_product(x1, x1)
    t = batch_product(x1, m)
    s2 = batch_product(s, s)
    x = 1.25 * x1 - 0.25 * batch_product(s2, t)
    return x * norm_values ** (-0.25)


def in_order(parts, index, size):
    ring = [parts[0]] + parts[:0:-1]
    ring = jnp.stack(ring + ring)
    return lax.dynamic_slice_in_dim(ring, size - index, size, 0)


def local(activations, cotangents, worker_of, left_stats):
    z, y = lax.axis_index("z"), lax.axis_index("y")
    x, c = lax.axis_index("x"), lax.axis_index("c")
    left = left_stats[0]
    block = jnp.arange(32, dtype=jnp.int32)
    slot_of = jnp.sum(
        ((worker_of[None, :] == worker_of[:, None]) & (block[None, :] < block[:, None])).astype(jnp.int32), axis=1
    )
    mine = z * 4 + y

    cots = jnp.transpose(cotangents, (1, 0, 2)).reshape(256, 256)
    cots_in = [shift(cots, "y", NY, o) for o in (1, 2, 3)]
    halves = [lax.dynamic_slice_in_dim(t, c * 128, 128, 0) for t in cots_in]
    others = [lax.dynamic_slice_in_dim(t, 128 - c * 128, 128, 0) for t in cots_in]
    cots_all = jnp.concatenate([cots] + halves + others, axis=0)
    got = []
    kept = None
    for k in (0, 1, 3, 2):
        first = ((z + k) % 4) * 2048
        own = lax.dynamic_slice(activations, (0, first + y * 512), (256, 512))
        pieces = []
        for o in (1, 2, 3):
            piece = lax.dynamic_slice(activations, (c * 128, first + ((y + o) % 4) * 512), (128, 512))
            pieces.append(shift(piece, "y", NY, o))
        direct = jnp.concatenate(pieces, axis=0)
        swapped = shift(direct, "c", NC, 1)
        acts = jnp.concatenate([own, direct, swapped], axis=0)
        part = jnp.einsum("tn,tf->nf", cots_all, acts, preferred_element_type=F32).reshape(2, 128, 512)
        matrix = ((z + k) % 8) // 4
        near, far = pick(part, matrix), pick(part, 1 - matrix)
        if k == 0:
            kept = near
        else:
            got.append(shift(near.astype(BF), "z", NZ, k))
        got.append(shift(far.astype(BF), "z", NZ, k + 4))
    total = kept
    for piece in got:
        total = total + piece.astype(F32)
    grad = total.astype(BF)

    occupied = jnp.stack([jnp.any((worker_of == mine) & (slot_of == s)) for s in range(2)]).astype(F32)
    roots = fourth_roots(left) * occupied[:, None, None]
    row = (c * 4 + x) * 64
    rows = lax.dynamic_slice(roots, (0, row, 0), (2, 64, 512)).astype(BF)
    items = jnp.stack([rows] + [shift(rows, "y", NY, o) for o in (1, 2, 3)]).reshape(8, 64, 512)
    routed = []
    for o in range(8):
        b = ((z + o) % 8) * 4 + y
        item = pick(items, ((y - worker_of[b] % 4) % 4) * 2 + slot_of[b])
        routed.append(item if o == 0 else shift(item, "z", NZ, o))
    mine_rows = pick(jnp.stack(routed), (z - worker_of[mine] // 4) % 8)
    by_x = in_order([mine_rows] + [shift(mine_rows, "x", NX, o) for o in (1, 2, 3)], x, NX).reshape(256, 512)
    by_c = shift(by_x, "c", NC, 1)
    root = jnp.where(c == 0, jnp.concatenate([by_x, by_c]), jnp.concatenate([by_c, by_x]))
    update = jnp.einsum("bc,kc->bk", root, grad, preferred_element_type=F32).astype(BF)

    gram = jnp.einsum("kb,kc->bc", grad, grad, preferred_element_type=F32) * (1.0 / KV)
    gram = gram.reshape(2, 256, 512)
    half = pick(gram, c) + shift(pick(gram, 1 - c).astype(BF), "c", NC, 1).astype(F32)
    half = half.reshape(4, 64, 512)
    quarter = pick(half, x)
    for o in (1, 2, 3):
        quarter = quarter + shift(pick(half, (x + o) % 4).astype(BF), "x", NX, o).astype(F32)
    quarter = quarter.astype(BF)
    column = jnp.stack([quarter] + [shift(quarter, "z", NZ, o) for o in range(1, 8)])
    blocks = jnp.arange(8, dtype=jnp.int32) * 4 + y
    arrived = None
    for o in range(4):
        target = z * 4 + (y + o) % 4
        pair = []
        for s in range(2):
            match = (worker_of[blocks] == target) & (slot_of[blocks] == s)
            source = jnp.sum(jnp.where(match, jnp.arange(8, dtype=jnp.int32), 0))
            item = pick(column, (z - source) % 8)
            pair.append(jnp.where(jnp.any(match), item, jnp.zeros((), BF)))
        pair = jnp.stack(pair)
        if o:
            pair = shift(pair, "y", NY, o)
        arrived = pair if arrived is None else arrived + pair
    by_x = in_order([arrived] + [shift(arrived, "x", NX, o) for o in (1, 2, 3)], x, NX)
    by_c = shift(by_x, "c", NC, 1)
    both = jnp.where(c == 0, jnp.stack([by_x, by_c]), jnp.stack([by_c, by_x]))
    gram_total = jnp.transpose(both, (2, 0, 1, 3, 4)).reshape(2, 512, 512).astype(F32)
    new_stats = (left + gram_total) * occupied[:, None, None]
    return new_stats[None], roots[None], update[None]


def solution(mesh):
    fine = Mesh(mesh.devices.reshape(NZ, NY, NX, NC), ("z", "y", "x", "c"))
    dp, mp = ("z", "y"), ("x", "c")
    return jax.shard_map(
        local,
        mesh=fine,
        in_specs=(P(dp, None), P(None, dp, mp), P(), P(dp, None, None, None)),
        out_specs=(P(dp, None, None, None), P(dp, None, None, None), P(dp, None, mp)),
        check_vma=False,
    )
```

```python
import functools

import jax
import jax.numpy as jnp
from jax import lax
from jax.experimental import pallas as pl
from jax.experimental.pallas import tpu as pltpu
from jax.sharding import Mesh, PartitionSpec as P

KV = 1024
NZ, NY, NX, NC = 8, 4, 4, 2
BF = jnp.bfloat16
F32 = jnp.float32
PAIRS = [(i, j) for i in range(4) for j in range(i, 4)]
SMEM = pl.BlockSpec(memory_space=pltpu.SMEM)
VMEM = pl.BlockSpec(memory_space=pltpu.VMEM)
HBM = pl.BlockSpec(memory_space=pltpu.HBM)
CHUNKS = ((0, 1, 2, 3),)


def vmem(mebibytes):
    return pltpu.CompilerParams(vmem_limit_bytes=mebibytes * 1024 * 1024)


TOKENS_FIRST = (((0,), (0,)), ((), ()))


def shift(x, axis, size, offset):
    return lax.ppermute(x, axis, [(i, (i + offset) % size) for i in range(size)])


def position():
    return [lax.axis_index(axis) for axis in ("z", "y", "x", "c")]


def struct(shape, dtype):
    return jax.ShapeDtypeStruct(shape, dtype)


def feature_block(place, k, offset):
    return ((place[0] + k) & 3) * 4 + ((place[1] + offset) & 3)


def pack_kernel(ks, with_cots, act, cot, *refs):
    outs, own, sems = refs[:3], refs[3], refs[4]
    place = position()
    c = place[3]
    copies = []
    for o in (1, 2, 3):
        out = outs[o - 1]
        for i, k in enumerate(ks):
            column = pl.multiple_of(feature_block(place, k, o) * 512, 512)
            source = act.at[pl.ds(pl.multiple_of(c * 128, 128), 128), pl.ds(column, 512)]
            copies.append((source, out.at[:, pl.ds(i * 512, 512)]))
        if with_cots:
            for h in range(2):
                for m in range(2):
                    lane = len(ks) * 512 + h * 256 + m * 128
                    copies.append((cot.at[m, pl.ds(h * 128, 128), :], out.at[:, pl.ds(lane, 128)]))
    for i, k in enumerate(ks):
        column = pl.multiple_of(feature_block(place, k, 0) * 512, 512)
        copies.append((act.at[:, pl.ds(column, 512)], own.at[:, pl.ds(i * 512, 512)]))
    started = []
    for n, (source, target) in enumerate(copies):
        copy = pltpu.make_async_copy(source, target, sems.at[n])
        copy.start()
        started.append(copy)
    for copy in started:
        copy.wait()


def pack(act, cot, ks, with_cots):
    width = len(ks) * 512 + (512 if with_cots else 0)
    count = 3 * (len(ks) + (4 if with_cots else 0)) + len(ks)
    return pl.pallas_call(
        functools.partial(pack_kernel, ks, with_cots),
        out_shape=[struct((128, width), BF)] * 3 + [struct((256, len(ks) * 512), BF)],
        in_specs=[HBM, HBM],
        out_specs=[VMEM] * 4,
        scratch_shapes=[pltpu.SemaphoreType.DMA((count,))],
        compiler_params=vmem(12),
        name="pack",
    )(act, cot)


def product_kernel(ks, lane0, own, cot, *refs):
    count = 2 * len(ks)
    cots, pieces, swaps, outs = refs[:3], refs[3:6], refs[6:9], refs[9 : 9 + count]
    lhs, acc = refs[9 + count :]
    z, _, _, c = position()
    near = pl.multiple_of(c * 256, 256)
    far = pl.multiple_of(256 - c * 256, 256)
    for m in range(2):
        lhs[pl.ds(m * 128, 128), pl.ds(0, 256)] = cot[m].T
    for o in range(3):
        for n, lane in enumerate((near, far)):
            lhs[:, pl.ds(256 + (2 * o + n) * 128, 128)] = cots[o][:, pl.ds(lane0 + lane, 256)].T
    for i, k in enumerate(ks):
        m = ((z + k) & 7) >> 2
        for half in range(2):
            column = pl.ds(i * 512 + half * 256, 256)
            total = jnp.dot(lhs[:, pl.ds(0, 256)], own[:, column], preferred_element_type=F32)
            for o in range(3):
                for n, piece in enumerate((pieces[o], swaps[o])):
                    left = lhs[:, pl.ds(256 + (2 * o + n) * 128, 128)]
                    total = total + jnp.dot(left, piece[:, column], preferred_element_type=F32)
            acc[...] = total
            for j, matrix in enumerate((m, 1 - m)):
                row = pl.multiple_of(matrix * 128, 128)
                out = outs[2 * i + j]
                out[:, pl.ds(half * 256, 256)] = acc[pl.ds(row, 128), :].astype(out.dtype)


def products(own, cot, cots, pieces, swaps, ks, lane0):
    types = [F32 if k == 0 and j == 0 else BF for k in ks for j in range(2)]
    return pl.pallas_call(
        functools.partial(product_kernel, ks, lane0),
        out_shape=[struct((128, 512), dtype) for dtype in types],
        in_specs=[VMEM] * 11,
        out_specs=[VMEM] * len(types),
        scratch_shapes=[pltpu.VMEM((256, 1024), BF), pltpu.VMEM((256, 256), F32)],
        compiler_params=vmem(16),
        cost_estimate=pl.CostEstimate(flops=2 * 512 * 256 * 1024 * len(ks), bytes_accessed=4 << 20, transcendentals=0),
        name="products",
    )(own, cot, *cots, *pieces, *swaps)


def mul(left, right):
    return jnp.dot(left.astype(BF), right.astype(BF), preferred_element_type=F32)


def plan_kernel(worker_of, plan):
    z, y, _, _ = position()
    for o in range(4):
        target = z * 4 + ((y + o) & 3)

        def step(b, state):
            count, first, second = state
            hit = worker_of[b] == target
            offset = jnp.where((b & 3) == y, b >> 2, -1)
            first = jnp.where(hit & (count == 0), offset, first)
            second = jnp.where(hit & (count == 1), offset, second)
            return count + hit.astype(jnp.int32), first, second

        none = jnp.int32(-1)
        _, first, second = lax.fori_loop(0, 32, step, (jnp.int32(0), none, none))
        plan[2 * o] = first
        plan[2 * o + 1] = second
        worker = worker_of[target]
        slot = lax.fori_loop(0, target, lambda b, n: n + (worker_of[b] == worker).astype(jnp.int32), jnp.int32(0))
        plan[8 + o] = jnp.where((worker & 3) == y, ((z - (worker >> 2)) & 7) * 2 + slot, -1)
    for n in range(12, 16):
        plan[n] = 0


def make_plan(worker_of):
    return pl.pallas_call(
        plan_kernel,
        out_shape=struct((16,), jnp.int32),
        in_specs=[SMEM],
        out_specs=SMEM,
        name="plan",
    )(worker_of)


def root_kernel(worker_of, left, root, strips, occupied):
    a = 1.5625
    slot = pl.program_id(0)
    z, y, x_place, c = position()
    mine = z * 4 + y
    count = lax.fori_loop(0, 32, lambda b, n: n + (worker_of[b] == mine).astype(jnp.int32), jnp.int32(0))
    matrix = left[0]
    norm = jnp.sqrt(jnp.sum(jnp.sum(matrix * matrix, axis=1, keepdims=True), axis=0, keepdims=True))
    m = matrix / norm
    m2 = mul(m, m)
    p = m2 * 0.0625 - m * 0.625
    u = m * 1.25 - m2 * 0.25
    q = p * (2 * a) + mul(p, p)
    v = u * (a * a) + mul(q, u)
    r = m * -0.3125 - v * 0.25
    s = r * (2 * a) + mul(r, r)
    t = m * a + mul(r, m)
    f = s * (2 * a * a) + mul(s, s)
    w = t * (a * a * a * a) + mul(f, t)
    held = (count > slot).astype(F32)
    occupied[0] = jnp.full((8, 128), held, F32)
    scale = lax.rsqrt(jnp.sqrt(norm)) * held
    row = lax.broadcasted_iota(jnp.int32, (512, 512), 0)
    column = lax.broadcasted_iota(jnp.int32, (512, 512), 1)
    x = jnp.where(row == column, 1.25 * a, 0.0) + r * 1.25 - w * 0.25
    root[0] = x * scale
    strip = c * 64 + x_place * 16
    for n, (i, j) in enumerate(PAIRS):
        rows = pl.ds(pl.multiple_of(i * 128 + strip, 16), 16)
        strips[0, n] = root[0, rows, pl.ds(j * 128, 128)].astype(BF)


def make_roots(worker_of, left):
    return pl.pallas_call(
        root_kernel,
        grid=(2,),
        out_shape=[struct((2, 512, 512), F32), struct((2, 10, 16, 128), BF), struct((2, 8, 128), F32)],
        in_specs=[SMEM, pl.BlockSpec((1, 512, 512), lambda s: (s, 0, 0))],
        out_specs=[pl.BlockSpec((1, 512, 512), lambda s: (s, 0, 0)), pl.BlockSpec((1, 10, 16, 128), lambda s: (s, 0, 0, 0)), pl.BlockSpec((1, 8, 128), lambda s: (s, 0, 0))],
        compiler_params=vmem(32),
        cost_estimate=pl.CostEstimate(flops=2 * 7 * 2 * 512**3, bytes_accessed=4 << 20, transcendentals=0),
        name="roots",
    )(worker_of, left)


def gram_kernel(mine, theirs, keep, send1, send2, send3, acc):
    _, _, x, c = position()
    for n, (i, j) in enumerate(PAIRS):
        total = 0.0
        for part in (mine, theirs):
            total = total + lax.dot_general(
                part[:, pl.ds(i * 128, 128)], part[:, pl.ds(j * 128, 128)], TOKENS_FIRST, preferred_element_type=F32
            )
        acc[n] = total * (1.0 / KV)
    for o, out in enumerate((keep, send1, send2, send3)):
        row = pl.multiple_of(c * 64 + ((x + o) & 3) * 16, 16)
        out[...] = acc[:, pl.ds(row, 16), :].astype(out.dtype)


def grams(mine, theirs):
    return pl.pallas_call(
        gram_kernel,
        out_shape=[struct((10, 16, 128), F32)] + [struct((10, 16, 128), BF)] * 3,
        in_specs=[VMEM, VMEM],
        out_specs=[VMEM] * 4,
        scratch_shapes=[pltpu.VMEM((10, 128, 128), F32)],
        compiler_params=vmem(8),
        name="grams",
    )(mine, theirs)


def choose_kernel(plan, column, *refs):
    roots, outs, held = refs[:8], refs[8:12], refs[12]
    for o in range(8):
        held[pl.ds(2 * o, 2)] = roots[o][...]
    for o in range(4):
        for s in range(2):
            index = plan[2 * o + s]
            item = column[jnp.maximum(index, 0)]
            outs[o][s] = jnp.where(index >= 0, item, jnp.zeros_like(item))
        index = plan[8 + o]
        item = held[jnp.maximum(index, 0)]
        outs[o][2] = jnp.where(index >= 0, item, jnp.zeros_like(item))


def choose(plan, roots, column):
    return pl.pallas_call(
        choose_kernel,
        out_shape=[struct((3, 10, 16, 128), BF)] * 4,
        in_specs=[SMEM] + [VMEM] * 9,
        out_specs=[VMEM] * 4,
        scratch_shapes=[pltpu.VMEM((16, 10, 16, 128), BF)],
        compiler_params=vmem(8),
        name="choose",
    )(plan, column, *roots)


def finish_kernel(left, occupied, grad, *refs):
    mine, theirs, (stats, update, whole, root) = refs[:4], refs[4:8], refs[8:]
    slot = pl.program_id(0)
    _, _, x, c = position()

    @pl.when(slot == 0)
    def _():
        for side, part in ((c, mine), (1 - c, theirs)):
            for o in range(4):
                row = pl.multiple_of(side * 64 + ((x - o) & 3) * 16, 16)
                whole[:, :, pl.ds(row, 16), :] = part[o][...]

    held = occupied[0, pl.ds(0, 1), :]
    for n, (i, j) in enumerate(PAIRS):
        block = whole[slot, n].astype(F32)
        above = (0, pl.ds(i * 128, 128), pl.ds(j * 128, 128))
        stats[above] = (left[above] + block) * held
        if i != j:
            below = (0, pl.ds(j * 128, 128), pl.ds(i * 128, 128))
            stats[below] = (left[below] + block.T) * held

    @pl.when(slot == 1)
    def _():
        for n, (i, j) in enumerate(PAIRS):
            block = whole[2, n]
            root[pl.ds(i * 128, 128), pl.ds(j * 128, 128)] = block
            if i != j:
                root[pl.ds(j * 128, 128), pl.ds(i * 128, 128)] = block.astype(F32).T.astype(BF)
        update[...] = lax.dot_general(
            root[...], grad[...], (((1,), (1,)), ((), ())), preferred_element_type=F32
        ).astype(BF)


def finish(left, occupied, grad, mine, theirs):
    by_slot = pl.BlockSpec((1, 512, 512), lambda s: (s, 0, 0))
    piece = pl.BlockSpec((3, 10, 16, 128), lambda s: (0, 0, 0, 0))
    return pl.pallas_call(
        finish_kernel,
        grid=(2,),
        out_shape=[struct((2, 512, 512), F32), struct((512, 128), BF)],
        in_specs=[by_slot, pl.BlockSpec((1, 8, 128), lambda s: (s, 0, 0)), pl.BlockSpec((128, 512), lambda s: (0, 0))]
        + [piece] * 8,
        out_specs=[by_slot, pl.BlockSpec((512, 128), lambda s: (0, 0))],
        scratch_shapes=[pltpu.VMEM((3, 10, 128, 128), BF), pltpu.VMEM((512, 512), BF)],
        compiler_params=vmem(16),
        name="finish",
    )(left, occupied, grad, *mine, *theirs)


def local(activations, cotangents, worker_of, left_stats):
    left = left_stats[0]

    packed = [pack(activations, cotangents, ks, n == 0) for n, ks in enumerate(CHUNKS)]
    sent = packed[0][:3]
    first = arriving = [shift(p, "y", NY, o + 1) for o, p in enumerate(sent)]
    later, _ = lax.optimization_barrier((left, sent))
    roots, strips, occupied = make_roots(worker_of, later)
    plan = make_plan(worker_of)
    root_strips = [strips] + [shift(strips, "z", NZ, o) for o in range(1, 8)]
    first, arriving, root_strips = lax.optimization_barrier((first, arriving, root_strips))
    got, kept = [], None
    for n, ks in enumerate(CHUNKS):
        if n + 1 < len(CHUNKS):
            arriving, sent = lax.optimization_barrier((arriving, packed[n + 1][:3]))
            following = [shift(p, "y", NY, o + 1) for o, p in enumerate(sent)]
        swapped = [shift(p, "c", NC, 1) for p in arriving]
        parts = products(packed[n][3], cotangents, first, arriving, swapped, ks, 512 * len(CHUNKS[0]))
        for i, k in enumerate(ks):
            near, far = parts[2 * i : 2 * i + 2]
            if k == 0:
                kept = near
            else:
                got.append(shift(near, "z", NZ, k))
            got.append(shift(far, "z", NZ, k + 4))
        if n + 1 < len(CHUNKS):
            arriving = following
    total = kept
    for piece in got:
        total = total + piece.astype(F32)
    grad = total.astype(BF)

    theirs = shift(grad, "c", NC, 1)
    strip, *sends = grams(grad, theirs)
    for o, send in enumerate(sends):
        strip = strip + shift(send, "x", NX, o + 1).astype(F32)
    strip = strip.astype(BF)
    column = lax.all_to_all(jnp.broadcast_to(strip[None], (8, 10, 16, 128)), "z", 0, 0, tiled=True)
    routed = choose(plan, root_strips, column)
    arrived = routed[0]
    for o in (1, 2, 3):
        arrived = arrived + shift(routed[o], "y", NY, o)
    by_x = [arrived] + [shift(arrived, "x", NX, o) for o in (1, 2, 3)]
    by_c = [shift(piece, "c", NC, 1) for piece in by_x]
    new_stats, update = finish(left, occupied, grad, by_x, by_c)
    return new_stats[None], roots[None], update[None]


def solution(mesh):
    fine = Mesh(mesh.devices.reshape(NZ, NY, NX, NC), ("z", "y", "x", "c"))
    dp, mp = ("z", "y"), ("x", "c")
    return jax.shard_map(
        local,
        mesh=fine,
        in_specs=(P(dp, None), P(None, dp, mp), P(), P(dp, None, None, None)),
        out_specs=(P(dp, None, None, None), P(dp, None, None, None), P(dp, None, mp)),
        check_vma=False,
    )
```

```python
import functools

import jax
import jax.numpy as jnp
from jax import lax
from jax.experimental import pallas as pl
from jax.experimental.pallas import tpu as pltpu
from jax.sharding import Mesh, PartitionSpec as P

KV = 1024
NZ, NY, NX, NC = 8, 4, 4, 2
BF = jnp.bfloat16
F32 = jnp.float32
PAIRS = [(i, j) for i in range(4) for j in range(i, 4)]
SMEM = pl.BlockSpec(memory_space=pltpu.SMEM)
VMEM = pl.BlockSpec(memory_space=pltpu.VMEM)
HBM = pl.BlockSpec(memory_space=pltpu.HBM)


def vmem(mebibytes):
    return pltpu.CompilerParams(vmem_limit_bytes=mebibytes * 1024 * 1024)


TOKENS_FIRST = (((0,), (0,)), ((), ()))


def shift(x, axis, size, offset):
    return lax.ppermute(x, axis, [(i, (i + offset) % size) for i in range(size)])


def position():
    return [lax.axis_index(axis) for axis in ("z", "y", "x", "c")]


def struct(shape, dtype):
    return jax.ShapeDtypeStruct(shape, dtype)


def feature_block(place, k, offset):
    return ((place[0] + k) & 3) * 4 + ((place[1] + offset) & 3)


def pack_kernel(act, cot, *refs):
    outs, sems = refs[:3], refs[3]
    place = position()
    half = pl.ds(pl.multiple_of(place[3] * 128, 128), 128)
    copies = []
    for o in (1, 2, 3):
        out = outs[o - 1]
        for k in range(4):
            column = pl.multiple_of(feature_block(place, k, o) * 512, 512)
            copies.append((act.at[half, pl.ds(column, 512)], out.at[:, pl.ds(k * 512, 512)]))
        for h in range(2):
            for m in range(2):
                lane = 2048 + h * 256 + m * 128
                copies.append((cot.at[m, pl.ds(h * 128, 128), :], out.at[:, pl.ds(lane, 128)]))
    started = []
    for n, (source, target) in enumerate(copies):
        copy = pltpu.make_async_copy(source, target, sems.at[n])
        copy.start()
        started.append(copy)
    for copy in started:
        copy.wait()


def pack(act, cot):
    return pl.pallas_call(
        pack_kernel,
        out_shape=[struct((128, 2560), BF)] * 3,
        in_specs=[HBM, HBM],
        out_specs=[VMEM] * 3,
        scratch_shapes=[pltpu.SemaphoreType.DMA((24,))],
        compiler_params=vmem(60),
        name="pack",
    )(act, cot)


def own_kernel(act, own, sems):
    place = position()
    copies = []
    for k in range(4):
        column = pl.multiple_of(feature_block(place, k, 0) * 512, 512)
        copies.append(pltpu.make_async_copy(act.at[:, pl.ds(column, 512)], own.at[:, pl.ds(k * 512, 512)], sems.at[k]))
        copies[k].start()
    for copy in copies:
        copy.wait()


def keep_own(act):
    return pl.pallas_call(
        own_kernel,
        out_shape=struct((256, 2048), BF),
        in_specs=[HBM],
        out_specs=VMEM,
        scratch_shapes=[pltpu.SemaphoreType.DMA((4,))],
        compiler_params=vmem(60),
        name="own",
    )(act)


def product_kernel(own, cot, *refs):
    pieces, swaps, (kept, two, six, up, down, half0, half1), (lhs, acc) = refs[:3], refs[3:6], refs[6:13], refs[13:]
    z, _, _, c = position()
    straight = pl.multiple_of(c * 256, 256)
    crossed = pl.multiple_of(256 - c * 256, 256)
    for m in range(2):
        lhs[pl.ds(m * 128, 128), pl.ds(0, 256)] = cot[m].T
    for o in range(3):
        for n, lane in enumerate((straight, crossed)):
            lhs[:, pl.ds(256 + (2 * o + n) * 128, 128)] = pieces[o][:, pl.ds(2048 + lane, 256)].T
    for k in range(4):
        m = ((z + k) & 7) >> 2
        for half in range(2):
            column = pl.ds(k * 512 + half * 256, 256)
            total = jnp.dot(lhs[:, pl.ds(0, 256)], own[:, column], preferred_element_type=F32)
            for o in range(3):
                for n, piece in enumerate((pieces[o], swaps[o])):
                    left = lhs[:, pl.ds(256 + (2 * o + n) * 128, 128)]
                    total = total + jnp.dot(left, piece[:, column], preferred_element_type=F32)
            acc[...] = total
            lanes = pl.ds(half * 256, 256)
            near = acc[pl.ds(pl.multiple_of(m * 128, 128), 128), :]
            far = acc[pl.ds(pl.multiple_of(128 - m * 128, 128), 128), :]
            if k == 0:
                kept[:, lanes] = near
                half0[:, lanes] = far[:64].astype(BF)
                half1[:, lanes] = far[64:].astype(BF)
            elif k == 2:
                two[:, lanes] = near
                six[:, lanes] = far
            else:
                up[k // 2, :, lanes] = near.astype(BF)
                down[1 - k // 2, :, lanes] = far.astype(BF)


def products(own, cot, pieces, swaps):
    return pl.pallas_call(
        product_kernel,
        out_shape=[struct((128, 512), F32)] * 3 + [struct((2, 128, 512), BF)] * 2 + [struct((64, 512), BF)] * 2,
        in_specs=[VMEM] * 8,
        out_specs=[VMEM] * 7,
        scratch_shapes=[pltpu.VMEM((256, 1024), BF), pltpu.VMEM((256, 256), F32)],
        compiler_params=vmem(8),
        cost_estimate=pl.CostEstimate(flops=2 * 2048 * 256 * 1024, bytes_accessed=4 << 20, transcendentals=0),
        name="products",
    )(own, cot, *pieces, *swaps)


def merge_kernel(two, six, up, down, low, high, ahead, back):
    ahead[pl.ds(0, 64), :] = (two[pl.ds(0, 64), :] + up[1, pl.ds(0, 64), :].astype(F32) + low[...].astype(F32)).astype(BF)
    ahead[pl.ds(64, 64), :] = (two[pl.ds(64, 64), :] + up[1, pl.ds(64, 64), :].astype(F32)).astype(BF)
    back[pl.ds(0, 64), :] = (six[pl.ds(0, 64), :] + down[1, pl.ds(0, 64), :].astype(F32)).astype(BF)
    back[pl.ds(64, 64), :] = (six[pl.ds(64, 64), :] + down[1, pl.ds(64, 64), :].astype(F32) + high[...].astype(F32)).astype(BF)


def merge(*parts):
    return pl.pallas_call(
        merge_kernel,
        out_shape=[struct((128, 512), BF)] * 2,
        in_specs=[VMEM] * 6,
        out_specs=[VMEM] * 2,
        compiler_params=vmem(6),
        name="merge",
    )(*parts)


def mul(left, right):
    return jnp.dot(left.astype(BF), right.astype(BF), preferred_element_type=F32)


def plan_kernel(worker_of, plan):
    z, y, _, _ = position()
    for o in range(4):
        target = z * 4 + ((y + o) & 3)

        def step(b, state):
            count, first, second = state
            hit = worker_of[b] == target
            offset = jnp.where((b & 3) == y, b >> 2, -1)
            first = jnp.where(hit & (count == 0), offset, first)
            second = jnp.where(hit & (count == 1), offset, second)
            return count + hit.astype(jnp.int32), first, second

        none = jnp.int32(-1)
        _, first, second = lax.fori_loop(0, 32, step, (jnp.int32(0), none, none))
        plan[2 * o] = first
        plan[2 * o + 1] = second
        worker = worker_of[target]
        slot = lax.fori_loop(0, target, lambda b, n: n + (worker_of[b] == worker).astype(jnp.int32), jnp.int32(0))
        plan[8 + o] = jnp.where((worker & 3) == y, (worker >> 2) * 2 + slot, -1)
    for n in range(12, 16):
        plan[n] = 0


def make_plan(worker_of):
    return pl.pallas_call(
        plan_kernel,
        out_shape=struct((16,), jnp.int32),
        in_specs=[SMEM],
        out_specs=SMEM,
        name="plan",
    )(worker_of)


def root_kernel(worker_of, left, root, strips, occupied):
    a = 1.5625
    slot = pl.program_id(0)
    z, y, x_place, c = position()
    mine = z * 4 + y
    count = lax.fori_loop(0, 32, lambda b, n: n + (worker_of[b] == mine).astype(jnp.int32), jnp.int32(0))
    matrix = left[0]
    norm = jnp.sqrt(jnp.sum(jnp.sum(matrix * matrix, axis=1, keepdims=True), axis=0, keepdims=True))
    m = matrix / norm
    m2 = mul(m, m)
    p = m2 * 0.0625 - m * 0.625
    u = m * 1.25 - m2 * 0.25
    q = p * (2 * a) + mul(p, p)
    v = u * (a * a) + mul(q, u)
    r = m * -0.3125 - v * 0.25
    s = r * (2 * a) + mul(r, r)
    t = m * a + mul(r, m)
    f = s * (2 * a * a) + mul(s, s)
    w = t * (a * a * a * a) + mul(f, t)
    held = (count > slot).astype(F32)
    occupied[0] = jnp.full((8, 128), held, F32)
    scale = lax.rsqrt(jnp.sqrt(norm)) * held
    row = lax.broadcasted_iota(jnp.int32, (512, 512), 0)
    column = lax.broadcasted_iota(jnp.int32, (512, 512), 1)
    x = jnp.where(row == column, 1.25 * a, 0.0) + r * 1.25 - w * 0.25
    root[0] = x * scale
    strip = c * 64 + x_place * 16
    for n, (i, j) in enumerate(PAIRS):
        rows = pl.ds(pl.multiple_of(i * 128 + strip, 16), 16)
        strips[0, n] = root[0, rows, pl.ds(j * 128, 128)].astype(BF)


def make_roots(worker_of, left):
    return pl.pallas_call(
        root_kernel,
        grid=(2,),
        out_shape=[struct((2, 512, 512), F32), struct((2, 10, 16, 128), BF), struct((2, 8, 128), F32)],
        in_specs=[SMEM, pl.BlockSpec((1, 512, 512), lambda s: (s, 0, 0))],
        out_specs=[pl.BlockSpec((1, 512, 512), lambda s: (s, 0, 0)), pl.BlockSpec((1, 10, 16, 128), lambda s: (s, 0, 0, 0)), pl.BlockSpec((1, 8, 128), lambda s: (s, 0, 0))],
        compiler_params=vmem(10),
        cost_estimate=pl.CostEstimate(flops=2 * 7 * 2 * 512**3, bytes_accessed=4 << 20, transcendentals=0),
        name="roots",
    )(worker_of, left)


def gram_kernel(mine, theirs, keep, send1, send2, send3, acc):
    _, _, x, c = position()
    for n, (i, j) in enumerate(PAIRS):
        total = 0.0
        for part in (mine, theirs):
            total = total + lax.dot_general(
                part[:, pl.ds(i * 128, 128)], part[:, pl.ds(j * 128, 128)], TOKENS_FIRST, preferred_element_type=F32
            )
        acc[n] = total * (1.0 / KV)
    for o, out in enumerate((keep, send1, send2, send3)):
        row = pl.multiple_of(c * 64 + ((x + o) & 3) * 16, 16)
        out[...] = acc[:, pl.ds(row, 16), :].astype(out.dtype)


def grams(mine, theirs):
    return pl.pallas_call(
        gram_kernel,
        out_shape=[struct((10, 16, 128), F32)] + [struct((10, 16, 128), BF)] * 3,
        in_specs=[VMEM, VMEM],
        out_specs=[VMEM] * 4,
        scratch_shapes=[pltpu.VMEM((10, 128, 128), F32)],
        compiler_params=vmem(8),
        name="grams",
    )(mine, theirs)


def choose_kernel(plan, roots, column, *outs):
    for o in range(4):
        for s in range(2):
            index = plan[2 * o + s]
            item = column[jnp.maximum(index, 0)]
            outs[o][s] = jnp.where(index >= 0, item, jnp.zeros_like(item))
        index = plan[8 + o]
        item = roots[jnp.maximum(index, 0)]
        outs[o][2] = jnp.where(index >= 0, item, jnp.zeros_like(item))


def choose(plan, roots, column):
    return pl.pallas_call(
        choose_kernel,
        out_shape=[struct((3, 10, 16, 128), BF)] * 4,
        in_specs=[SMEM, VMEM, VMEM],
        out_specs=[VMEM] * 4,
        compiler_params=vmem(8),
        name="choose",
    )(plan, roots, column)


def finish_kernel(left, occupied, grad, *refs):
    mine, theirs, (stats, update, whole, root) = refs[:4], refs[4:8], refs[8:]
    slot = pl.program_id(0)
    _, _, x, c = position()

    @pl.when(slot == 0)
    def _():
        for side, part in ((c, mine), (1 - c, theirs)):
            for o in range(4):
                row = pl.multiple_of(side * 64 + ((x - o) & 3) * 16, 16)
                whole[:, :, pl.ds(row, 16), :] = part[o][...]

    held = occupied[0, pl.ds(0, 1), :]
    for n, (i, j) in enumerate(PAIRS):
        block = whole[slot, n].astype(F32)
        above = (0, pl.ds(i * 128, 128), pl.ds(j * 128, 128))
        stats[above] = (left[above] + block) * held
        if i != j:
            below = (0, pl.ds(j * 128, 128), pl.ds(i * 128, 128))
            stats[below] = (left[below] + block.T) * held

    @pl.when(slot == 1)
    def _():
        for n, (i, j) in enumerate(PAIRS):
            block = whole[2, n]
            root[pl.ds(i * 128, 128), pl.ds(j * 128, 128)] = block
            if i != j:
                root[pl.ds(j * 128, 128), pl.ds(i * 128, 128)] = block.astype(F32).T.astype(BF)
        update[...] = lax.dot_general(
            root[...], grad[...], (((1,), (1,)), ((), ())), preferred_element_type=F32
        ).astype(BF)


def finish(left, occupied, grad, mine, theirs):
    by_slot = pl.BlockSpec((1, 512, 512), lambda s: (s, 0, 0))
    piece = pl.BlockSpec((3, 10, 16, 128), lambda s: (0, 0, 0, 0))
    return pl.pallas_call(
        finish_kernel,
        grid=(2,),
        out_shape=[struct((2, 512, 512), F32), struct((512, 128), BF)],
        in_specs=[by_slot, pl.BlockSpec((1, 8, 128), lambda s: (s, 0, 0)), pl.BlockSpec((128, 512), lambda s: (0, 0))]
        + [piece] * 8,
        out_specs=[by_slot, pl.BlockSpec((512, 128), lambda s: (0, 0))],
        scratch_shapes=[pltpu.VMEM((3, 10, 128, 128), BF), pltpu.VMEM((512, 512), BF)],
        compiler_params=vmem(10),
        name="finish",
    )(left, occupied, grad, *mine, *theirs)


def local(activations, cotangents, worker_of, left_stats):
    left = left_stats[0]

    sent = pack(activations, cotangents)
    arrived = [shift(p, "y", NY, o + 1) for o, p in enumerate(sent)]
    later, _ = lax.optimization_barrier((left, sent))
    roots, strips, occupied = make_roots(worker_of, later)
    plan = make_plan(worker_of)
    root_strips = lax.all_to_all(jnp.broadcast_to(strips[None], (8, 2, 10, 16, 128)), "z", 0, 0, tiled=True)
    later, _ = lax.optimization_barrier((activations, plan))
    own = keep_own(later)
    arrived, strips, plan, own = lax.optimization_barrier((arrived, strips, plan, own))
    swapped = [shift(p, "c", NC, 1) for p in arrived]
    swapped, root_strips = lax.optimization_barrier((swapped, root_strips))
    kept, two, six, up, down, half0, half1 = products(own, cotangents, arrived, swapped)
    up, down = shift(up, "z", NZ, 1), shift(down, "z", NZ, 7)
    ahead, back = merge(two, six, up, down, shift(half0, "z", NZ, 2), shift(half1, "z", NZ, 6))
    total = kept + up[0].astype(F32) + down[0].astype(F32)
    total = total + shift(ahead, "z", NZ, 2).astype(F32) + shift(back, "z", NZ, 6).astype(F32)
    grad = total.astype(BF)

    theirs = shift(grad, "c", NC, 1)
    strip, *sends = grams(grad, theirs)
    for o, send in enumerate(sends):
        strip = strip + shift(send, "x", NX, o + 1).astype(F32)
    strip = strip.astype(BF)
    column = lax.all_to_all(jnp.broadcast_to(strip[None], (8, 10, 16, 128)), "z", 0, 0, tiled=True)
    routed = choose(plan, root_strips.reshape(16, 10, 16, 128), column)
    arrived = routed[0]
    for o in (1, 2, 3):
        arrived = arrived + shift(routed[o], "y", NY, o)
    by_x = [arrived] + [shift(arrived, "x", NX, o) for o in (1, 2, 3)]
    by_c = [shift(piece, "c", NC, 1) for piece in by_x]
    new_stats, update = finish(left, occupied, grad, by_x, by_c)
    return new_stats[None], roots[None], update[None]


def solution(mesh):
    fine = Mesh(mesh.devices.reshape(NZ, NY, NX, NC), ("z", "y", "x", "c"))
    dp, mp = ("z", "y"), ("x", "c")
    return jax.shard_map(
        local,
        mesh=fine,
        in_specs=(P(dp, None), P(None, dp, mp), P(), P(dp, None, None, None)),
        out_specs=(P(dp, None, None, None), P(dp, None, None, None), P(dp, None, mp)),
        check_vma=False,
    )
```

```python
import functools

import jax
import jax.numpy as jnp
from jax import lax
from jax.experimental import pallas as pl
from jax.experimental.pallas import tpu as pltpu
from jax.sharding import Mesh, PartitionSpec as P

KV = 1024
NZ, NY, NX, NC = 8, 4, 4, 2
BF = jnp.bfloat16
F32 = jnp.float32
PAIRS = [(i, j) for i in range(4) for j in range(i, 4)]
SMEM = pl.BlockSpec(memory_space=pltpu.SMEM)
VMEM = pl.BlockSpec(memory_space=pltpu.VMEM)
HBM = pl.BlockSpec(memory_space=pltpu.HBM)


def vmem(mebibytes):
    return pltpu.CompilerParams(vmem_limit_bytes=mebibytes * 1024 * 1024)


TOKENS_FIRST = (((0,), (0,)), ((), ()))


def shift(x, axis, size, offset):
    return lax.ppermute(x, axis, [(i, (i + offset) % size) for i in range(size)])


def position():
    return [lax.axis_index(axis) for axis in ("z", "y", "x", "c")]


def struct(shape, dtype):
    return jax.ShapeDtypeStruct(shape, dtype)


def feature_block(place, k, offset):
    return ((place[0] + k) & 3) * 4 + ((place[1] + offset) & 3)


def pack_kernel(act, cot, *refs):
    outs, sems = refs[:3], refs[3]
    place = position()
    half = pl.ds(pl.multiple_of(place[3] * 128, 128), 128)
    copies = []
    for o in (1, 2, 3):
        out = outs[o - 1]
        for k in range(4):
            column = pl.multiple_of(feature_block(place, k, o) * 512, 512)
            copies.append((act.at[half, pl.ds(column, 512)], out.at[:, pl.ds(k * 512, 512)]))
        for h in range(2):
            for m in range(2):
                lane = 2048 + h * 256 + m * 128
                copies.append((cot.at[m, pl.ds(h * 128, 128), :], out.at[:, pl.ds(lane, 128)]))
    started = []
    for n, (source, target) in enumerate(copies):
        copy = pltpu.make_async_copy(source, target, sems.at[n])
        copy.start()
        started.append(copy)
    for copy in started:
        copy.wait()


def pack(act, cot):
    return pl.pallas_call(
        pack_kernel,
        out_shape=[struct((128, 2560), BF)] * 3,
        in_specs=[HBM, HBM],
        out_specs=[VMEM] * 3,
        scratch_shapes=[pltpu.SemaphoreType.DMA((24,))],
        compiler_params=vmem(60),
        name="pack",
    )(act, cot)


def own_kernel(act, own, sems):
    place = position()
    copies = []
    for k in range(4):
        column = pl.multiple_of(feature_block(place, k, 0) * 512, 512)
        copies.append(pltpu.make_async_copy(act.at[:, pl.ds(column, 512)], own.at[:, pl.ds(k * 512, 512)], sems.at[k]))
        copies[k].start()
    for copy in copies:
        copy.wait()


def keep_own(act):
    return pl.pallas_call(
        own_kernel,
        out_shape=struct((256, 2048), BF),
        in_specs=[HBM],
        out_specs=VMEM,
        scratch_shapes=[pltpu.SemaphoreType.DMA((4,))],
        compiler_params=vmem(8),
        name="own",
    )(act)


def first_kernel(own, cot, *refs):
    pieces, acc, crossed, lhs = refs[:3], refs[3], refs[4], refs[5]
    c = position()[3]
    straight = pl.multiple_of(c * 256, 256)
    other = pl.multiple_of(256 - c * 256, 256)
    for m in range(2):
        lhs[pl.ds(m * 128, 128), pl.ds(0, 256)] = cot[m].T
    for o in range(3):
        lhs[:, pl.ds(256 + o * 128, 128)] = pieces[o][:, pl.ds(2048 + straight, 256)].T
        crossed[:, pl.ds(o * 128, 128)] = pieces[o][:, pl.ds(2048 + other, 256)].T
    for n in range(8):
        column = pl.ds(n * 256, 256)
        total = jnp.dot(lhs[:, pl.ds(0, 256)], own[:, column], preferred_element_type=F32)
        for o in range(3):
            left = lhs[:, pl.ds(256 + o * 128, 128)]
            total = total + jnp.dot(left, pieces[o][:, column], preferred_element_type=F32)
        acc[:, column] = total


def first_products(own, cot, pieces):
    return pl.pallas_call(
        first_kernel,
        out_shape=[struct((256, 2048), F32), struct((256, 384), BF)],
        in_specs=[VMEM] * 5,
        out_specs=[VMEM] * 2,
        scratch_shapes=[pltpu.VMEM((256, 640), BF)],
        compiler_params=vmem(10),
        cost_estimate=pl.CostEstimate(flops=2048 * 256 * 1024, bytes_accessed=4 << 20, transcendentals=0),
        name="first",
    )(own, cot, *pieces)


def second_kernel(acc, crossed, *refs):
    swaps, (kept, two, six, up, down, half0, half1, total) = refs[:3], refs[3:]
    z = position()[0]
    for k in range(4):
        m = ((z + k) & 7) >> 2
        for half in range(2):
            column = pl.ds(k * 512 + half * 256, 256)
            value = acc[:, column]
            for o in range(3):
                value = value + jnp.dot(
                    crossed[:, pl.ds(o * 128, 128)], swaps[o][:, column], preferred_element_type=F32
                )
            total[...] = value
            lanes = pl.ds(half * 256, 256)
            near = total[pl.ds(pl.multiple_of(m * 128, 128), 128), :]
            far = total[pl.ds(pl.multiple_of(128 - m * 128, 128), 128), :]
            if k == 0:
                kept[:, lanes] = near
                half0[:, lanes] = far[:64].astype(BF)
                half1[:, lanes] = far[64:].astype(BF)
            elif k == 2:
                two[:, lanes] = near
                six[:, lanes] = far
            else:
                up[k // 2, :, lanes] = near.astype(BF)
                down[1 - k // 2, :, lanes] = far.astype(BF)


def second_products(acc, crossed, swaps):
    return pl.pallas_call(
        second_kernel,
        out_shape=[struct((128, 512), F32)] * 3 + [struct((2, 128, 512), BF)] * 2 + [struct((64, 512), BF)] * 2,
        in_specs=[VMEM] * 5,
        out_specs=[VMEM] * 7,
        scratch_shapes=[pltpu.VMEM((256, 256), F32)],
        compiler_params=vmem(10),
        cost_estimate=pl.CostEstimate(flops=2048 * 256 * 1024, bytes_accessed=4 << 20, transcendentals=0),
        name="second",
    )(acc, crossed, *swaps)


def merge_kernel(two, six, up, down, low, high, ahead, back):
    ahead[pl.ds(0, 64), :] = (two[pl.ds(0, 64), :] + up[1, pl.ds(0, 64), :].astype(F32) + low[...].astype(F32)).astype(BF)
    ahead[pl.ds(64, 64), :] = (two[pl.ds(64, 64), :] + up[1, pl.ds(64, 64), :].astype(F32)).astype(BF)
    back[pl.ds(0, 64), :] = (six[pl.ds(0, 64), :] + down[1, pl.ds(0, 64), :].astype(F32)).astype(BF)
    back[pl.ds(64, 64), :] = (six[pl.ds(64, 64), :] + down[1, pl.ds(64, 64), :].astype(F32) + high[...].astype(F32)).astype(BF)


def merge(*parts):
    return pl.pallas_call(
        merge_kernel,
        out_shape=[struct((128, 512), BF)] * 2,
        in_specs=[VMEM] * 6,
        out_specs=[VMEM] * 2,
        compiler_params=vmem(6),
        name="merge",
    )(*parts)


def mul(left, right):
    return jnp.dot(left.astype(BF), right.astype(BF), preferred_element_type=F32)


def plan_kernel(worker_of, plan):
    z, y, _, _ = position()
    for o in range(4):
        target = z * 4 + ((y + o) & 3)

        def step(b, state):
            count, first, second = state
            hit = worker_of[b] == target
            offset = jnp.where((b & 3) == y, b >> 2, -1)
            first = jnp.where(hit & (count == 0), offset, first)
            second = jnp.where(hit & (count == 1), offset, second)
            return count + hit.astype(jnp.int32), first, second

        none = jnp.int32(-1)
        _, first, second = lax.fori_loop(0, 32, step, (jnp.int32(0), none, none))
        plan[2 * o] = first
        plan[2 * o + 1] = second
        worker = worker_of[target]
        slot = lax.fori_loop(0, target, lambda b, n: n + (worker_of[b] == worker).astype(jnp.int32), jnp.int32(0))
        plan[8 + o] = jnp.where((worker & 3) == y, (worker >> 2) * 2 + slot, -1)
    for n in range(12, 16):
        plan[n] = 0


def make_plan(worker_of):
    return pl.pallas_call(
        plan_kernel,
        out_shape=struct((16,), jnp.int32),
        in_specs=[SMEM],
        out_specs=SMEM,
        name="plan",
    )(worker_of)


def root_kernel(worker_of, left, root, strips, occupied):
    a = 1.5625
    slot = pl.program_id(0)
    z, y, x_place, c = position()
    mine = z * 4 + y
    count = lax.fori_loop(0, 32, lambda b, n: n + (worker_of[b] == mine).astype(jnp.int32), jnp.int32(0))
    matrix = left[0]
    norm = jnp.sqrt(jnp.sum(jnp.sum(matrix * matrix, axis=1, keepdims=True), axis=0, keepdims=True))
    m = matrix / norm
    m2 = mul(m, m)
    p = m2 * 0.0625 - m * 0.625
    u = m * 1.25 - m2 * 0.25
    q = p * (2 * a) + mul(p, p)
    v = u * (a * a) + mul(q, u)
    r = m * -0.3125 - v * 0.25
    s = r * (2 * a) + mul(r, r)
    t = m * a + mul(r, m)
    f = s * (2 * a * a) + mul(s, s)
    w = t * (a * a * a * a) + mul(f, t)
    held = (count > slot).astype(F32)
    occupied[0] = jnp.full((8, 128), held, F32)
    scale = lax.rsqrt(jnp.sqrt(norm)) * held
    row = lax.broadcasted_iota(jnp.int32, (512, 512), 0)
    column = lax.broadcasted_iota(jnp.int32, (512, 512), 1)
    x = jnp.where(row == column, 1.25 * a, 0.0) + r * 1.25 - w * 0.25
    root[0] = x * scale
    strip = c * 64 + x_place * 16
    for n, (i, j) in enumerate(PAIRS):
        rows = pl.ds(pl.multiple_of(i * 128 + strip, 16), 16)
        strips[0, n] = root[0, rows, pl.ds(j * 128, 128)].astype(BF)


def make_roots(worker_of, left):
    return pl.pallas_call(
        root_kernel,
        grid=(2,),
        out_shape=[struct((2, 512, 512), F32), struct((2, 10, 16, 128), BF), struct((2, 8, 128), F32)],
        in_specs=[SMEM, pl.BlockSpec((1, 512, 512), lambda s: (s, 0, 0))],
        out_specs=[pl.BlockSpec((1, 512, 512), lambda s: (s, 0, 0)), pl.BlockSpec((1, 10, 16, 128), lambda s: (s, 0, 0, 0)), pl.BlockSpec((1, 8, 128), lambda s: (s, 0, 0))],
        compiler_params=vmem(10),
        cost_estimate=pl.CostEstimate(flops=2 * 7 * 2 * 512**3, bytes_accessed=4 << 20, transcendentals=0),
        name="roots",
    )(worker_of, left)


def gram_kernel(mine, theirs, keep, send1, send2, send3, acc):
    _, _, x, c = position()
    for n, (i, j) in enumerate(PAIRS):
        total = 0.0
        for part in (mine, theirs):
            total = total + lax.dot_general(
                part[:, pl.ds(i * 128, 128)], part[:, pl.ds(j * 128, 128)], TOKENS_FIRST, preferred_element_type=F32
            )
        acc[n] = total * (1.0 / KV)
    for o, out in enumerate((keep, send1, send2, send3)):
        row = pl.multiple_of(c * 64 + ((x + o) & 3) * 16, 16)
        out[...] = acc[:, pl.ds(row, 16), :].astype(out.dtype)


def grams(mine, theirs):
    return pl.pallas_call(
        gram_kernel,
        out_shape=[struct((10, 16, 128), F32)] + [struct((10, 16, 128), BF)] * 3,
        in_specs=[VMEM, VMEM],
        out_specs=[VMEM] * 4,
        scratch_shapes=[pltpu.VMEM((10, 128, 128), F32)],
        compiler_params=vmem(8),
        name="grams",
    )(mine, theirs)


def choose_kernel(plan, roots, column, *outs):
    for o in range(4):
        for s in range(2):
            index = plan[2 * o + s]
            item = column[jnp.maximum(index, 0)]
            outs[o][s] = jnp.where(index >= 0, item, jnp.zeros_like(item))
        index = plan[8 + o]
        item = roots[jnp.maximum(index, 0)]
        outs[o][2] = jnp.where(index >= 0, item, jnp.zeros_like(item))


def choose(plan, roots, column):
    return pl.pallas_call(
        choose_kernel,
        out_shape=[struct((3, 10, 16, 128), BF)] * 4,
        in_specs=[SMEM, VMEM, VMEM],
        out_specs=[VMEM] * 4,
        compiler_params=vmem(8),
        name="choose",
    )(plan, roots, column)


def finish_kernel(left, occupied, grad, *refs):
    mine, theirs, (stats, update, whole, root) = refs[:4], refs[4:8], refs[8:]
    slot = pl.program_id(0)
    _, _, x, c = position()

    @pl.when(slot == 0)
    def _():
        for side, part in ((c, mine), (1 - c, theirs)):
            for o in range(4):
                row = pl.multiple_of(side * 64 + ((x - o) & 3) * 16, 16)
                whole[:, :, pl.ds(row, 16), :] = part[o][...]

    held = occupied[0, pl.ds(0, 1), :]
    for n, (i, j) in enumerate(PAIRS):
        block = whole[slot, n].astype(F32)
        above = (0, pl.ds(i * 128, 128), pl.ds(j * 128, 128))
        stats[above] = (left[above] + block) * held
        if i != j:
            below = (0, pl.ds(j * 128, 128), pl.ds(i * 128, 128))
            stats[below] = (left[below] + block.T) * held

    @pl.when(slot == 1)
    def _():
        for n, (i, j) in enumerate(PAIRS):
            block = whole[2, n]
            root[pl.ds(i * 128, 128), pl.ds(j * 128, 128)] = block
            if i != j:
                root[pl.ds(j * 128, 128), pl.ds(i * 128, 128)] = block.astype(F32).T.astype(BF)
        update[...] = lax.dot_general(
            root[...], grad[...], (((1,), (1,)), ((), ())), preferred_element_type=F32
        ).astype(BF)


def finish(left, occupied, grad, mine, theirs):
    by_slot = pl.BlockSpec((1, 512, 512), lambda s: (s, 0, 0))
    piece = pl.BlockSpec((3, 10, 16, 128), lambda s: (0, 0, 0, 0))
    return pl.pallas_call(
        finish_kernel,
        grid=(2,),
        out_shape=[struct((2, 512, 512), F32), struct((512, 128), BF)],
        in_specs=[by_slot, pl.BlockSpec((1, 8, 128), lambda s: (s, 0, 0)), pl.BlockSpec((128, 512), lambda s: (0, 0))]
        + [piece] * 8,
        out_specs=[by_slot, pl.BlockSpec((512, 128), lambda s: (0, 0))],
        scratch_shapes=[pltpu.VMEM((3, 10, 128, 128), BF), pltpu.VMEM((512, 512), BF)],
        compiler_params=vmem(10),
        name="finish",
    )(left, occupied, grad, *mine, *theirs)


def local(activations, cotangents, worker_of, left_stats):
    left = left_stats[0]

    sent = pack(activations, cotangents)
    arrived = [shift(p, "y", NY, o + 1) for o, p in enumerate(sent)]
    later, _ = lax.optimization_barrier((left, sent))
    roots, strips, occupied = make_roots(worker_of, later)
    plan = make_plan(worker_of)
    root_strips = lax.all_to_all(jnp.broadcast_to(strips[None], (8, 2, 10, 16, 128)), "z", 0, 0, tiled=True)
    later, _ = lax.optimization_barrier((activations, plan))
    own = keep_own(later)
    arrived, strips, plan, own = lax.optimization_barrier((arrived, strips, plan, own))
    swapped = [shift(p, "c", NC, 1) for p in arrived]
    acc, crossed = first_products(own, cotangents, arrived)
    kept, two, six, up, down, half0, half1 = second_products(acc, crossed, swapped)
    up, down = shift(up, "z", NZ, 1), shift(down, "z", NZ, 7)
    ahead, back = merge(two, six, up, down, shift(half0, "z", NZ, 2), shift(half1, "z", NZ, 6))
    kept, root_strips = lax.optimization_barrier((kept, root_strips))
    total = kept + up[0].astype(F32) + down[0].astype(F32)
    total = total + shift(ahead, "z", NZ, 2).astype(F32) + shift(back, "z", NZ, 6).astype(F32)
    grad = total.astype(BF)

    theirs = shift(grad, "c", NC, 1)
    strip, *sends = grams(grad, theirs)
    for o, send in enumerate(sends):
        strip = strip + shift(send, "x", NX, o + 1).astype(F32)
    strip = strip.astype(BF)
    column = lax.all_to_all(jnp.broadcast_to(strip[None], (8, 10, 16, 128)), "z", 0, 0, tiled=True)
    routed = choose(plan, root_strips.reshape(16, 10, 16, 128), column)
    arrived = routed[0]
    for o in (1, 2, 3):
        arrived = arrived + shift(routed[o], "y", NY, o)
    by_x = [arrived] + [shift(arrived, "x", NX, o) for o in (1, 2, 3)]
    by_c = [shift(piece, "c", NC, 1) for piece in by_x]
    new_stats, update = finish(left, occupied, grad, by_x, by_c)
    return new_stats[None], roots[None], update[None]


def solution(mesh):
    fine = Mesh(mesh.devices.reshape(NZ, NY, NX, NC), ("z", "y", "x", "c"))
    dp, mp = ("z", "y"), ("x", "c")
    return jax.shard_map(
        local,
        mesh=fine,
        in_specs=(P(dp, None), P(None, dp, mp), P(), P(dp, None, None, None)),
        out_specs=(P(dp, None, None, None), P(dp, None, None, None), P(dp, None, mp)),
        check_vma=False,
    )
```

```python
import functools

import jax
import jax.numpy as jnp
from jax import lax
from jax.experimental import pallas as pl
from jax.experimental.pallas import tpu as pltpu
from jax.sharding import Mesh, PartitionSpec as P

KV = 1024
NZ, NY, NX, NC = 8, 4, 4, 2
BF = jnp.bfloat16
F32 = jnp.float32
PAIRS = [(i, j) for i in range(4) for j in range(i, 4)]
SMEM = pl.BlockSpec(memory_space=pltpu.SMEM)
VMEM = pl.BlockSpec(memory_space=pltpu.VMEM)
HBM = pl.BlockSpec(memory_space=pltpu.HBM)


def vmem(mebibytes):
    return pltpu.CompilerParams(vmem_limit_bytes=mebibytes * 1024 * 1024)


TOKENS_FIRST = (((0,), (0,)), ((), ()))


def shift(x, axis, size, offset):
    return lax.ppermute(x, axis, [(i, (i + offset) % size) for i in range(size)])


def position():
    return [lax.axis_index(axis) for axis in ("z", "y", "x", "c")]


def struct(shape, dtype):
    return jax.ShapeDtypeStruct(shape, dtype)


def feature_block(place, k, offset):
    return ((place[0] + k) & 3) * 4 + ((place[1] + offset) & 3)


def pack_kernel(act, cot, *refs):
    outs, sems = refs[:3], refs[3]
    place = position()
    half = pl.ds(pl.multiple_of(place[3] * 128, 128), 128)
    copies = []
    for o in (1, 2, 3):
        out = outs[o - 1]
        for k in range(4):
            column = pl.multiple_of(feature_block(place, k, o) * 512, 512)
            copies.append((act.at[half, pl.ds(column, 512)], out.at[:, pl.ds(k * 512, 512)]))
        for h in range(2):
            for m in range(2):
                lane = 2048 + h * 256 + m * 128
                copies.append((cot.at[m, pl.ds(h * 128, 128), :], out.at[:, pl.ds(lane, 128)]))
    started = []
    for n, (source, target) in enumerate(copies):
        copy = pltpu.make_async_copy(source, target, sems.at[n])
        copy.start()
        started.append(copy)
    for copy in started:
        copy.wait()


def pack(act, cot):
    return pl.pallas_call(
        pack_kernel,
        out_shape=[struct((128, 2560), BF)] * 3,
        in_specs=[HBM, HBM],
        out_specs=[VMEM] * 3,
        scratch_shapes=[pltpu.SemaphoreType.DMA((24,))],
        compiler_params=vmem(60),
        name="pack",
    )(act, cot)


def own_kernel(act, own, sems):
    place = position()
    copies = []
    for k in range(4):
        column = pl.multiple_of(feature_block(place, k, 0) * 512, 512)
        copies.append(pltpu.make_async_copy(act.at[:, pl.ds(column, 512)], own.at[:, pl.ds(k * 512, 512)], sems.at[k]))
        copies[k].start()
    for copy in copies:
        copy.wait()


def keep_own(act):
    return pl.pallas_call(
        own_kernel,
        out_shape=struct((256, 2048), BF),
        in_specs=[HBM],
        out_specs=VMEM,
        scratch_shapes=[pltpu.SemaphoreType.DMA((4,))],
        compiler_params=vmem(8),
        name="own",
    )(act)


def first_kernel(own, cot, *refs):
    pieces, acc, crossed, lhs = refs[:3], refs[3], refs[4], refs[5]
    c = position()[3]
    straight = pl.multiple_of(c * 256, 256)
    other = pl.multiple_of(256 - c * 256, 256)
    for m in range(2):
        lhs[pl.ds(m * 128, 128), pl.ds(0, 256)] = cot[m].T
    for o in range(3):
        lhs[:, pl.ds(256 + o * 128, 128)] = pieces[o][:, pl.ds(2048 + straight, 256)].T
        crossed[:, pl.ds(o * 128, 128)] = pieces[o][:, pl.ds(2048 + other, 256)].T
    for n in range(8):
        column = pl.ds(n * 256, 256)
        total = jnp.dot(lhs[:, pl.ds(0, 256)], own[:, column], preferred_element_type=F32)
        for o in range(3):
            left = lhs[:, pl.ds(256 + o * 128, 128)]
            total = total + jnp.dot(left, pieces[o][:, column], preferred_element_type=F32)
        acc[:, column] = total


def first_products(own, cot, pieces):
    return pl.pallas_call(
        first_kernel,
        out_shape=[struct((256, 2048), F32), struct((256, 384), BF)],
        in_specs=[VMEM] * 5,
        out_specs=[VMEM] * 2,
        scratch_shapes=[pltpu.VMEM((256, 640), BF)],
        compiler_params=vmem(10),
        cost_estimate=pl.CostEstimate(flops=2048 * 256 * 1024, bytes_accessed=4 << 20, transcendentals=0),
        name="first",
    )(own, cot, *pieces)


def second_kernel(acc, crossed, *refs):
    swaps, (kept, two, six, up, down, half0, half1, total) = refs[:3], refs[3:]
    z = position()[0]
    for k in range(4):
        m = ((z + k) & 7) >> 2
        for half in range(2):
            column = pl.ds(k * 512 + half * 256, 256)
            value = acc[:, column]
            for o in range(3):
                value = value + jnp.dot(
                    crossed[:, pl.ds(o * 128, 128)], swaps[o][:, column], preferred_element_type=F32
                )
            total[...] = value
            lanes = pl.ds(half * 256, 256)
            near = total[pl.ds(pl.multiple_of(m * 128, 128), 128), :]
            far = total[pl.ds(pl.multiple_of(128 - m * 128, 128), 128), :]
            if k == 0:
                kept[:, lanes] = near
                half0[:, lanes] = far[:64].astype(BF)
                half1[:, lanes] = far[64:].astype(BF)
            elif k == 2:
                two[:, lanes] = near
                six[:, lanes] = far
            else:
                up[k // 2, :, lanes] = near.astype(BF)
                down[1 - k // 2, :, lanes] = far.astype(BF)


def second_products(acc, crossed, swaps):
    return pl.pallas_call(
        second_kernel,
        out_shape=[struct((128, 512), F32)] * 3 + [struct((2, 128, 512), BF)] * 2 + [struct((64, 512), BF)] * 2,
        in_specs=[VMEM] * 5,
        out_specs=[VMEM] * 7,
        scratch_shapes=[pltpu.VMEM((256, 256), F32)],
        compiler_params=vmem(10),
        cost_estimate=pl.CostEstimate(flops=2048 * 256 * 1024, bytes_accessed=4 << 20, transcendentals=0),
        name="second",
    )(acc, crossed, *swaps)


def merge_kernel(two, six, up, down, low, high, ahead, back):
    ahead[pl.ds(0, 64), :] = (two[pl.ds(0, 64), :] + up[1, pl.ds(0, 64), :].astype(F32) + low[...].astype(F32)).astype(BF)
    ahead[pl.ds(64, 64), :] = (two[pl.ds(64, 64), :] + up[1, pl.ds(64, 64), :].astype(F32)).astype(BF)
    back[pl.ds(0, 64), :] = (six[pl.ds(0, 64), :] + down[1, pl.ds(0, 64), :].astype(F32)).astype(BF)
    back[pl.ds(64, 64), :] = (six[pl.ds(64, 64), :] + down[1, pl.ds(64, 64), :].astype(F32) + high[...].astype(F32)).astype(BF)


def merge(*parts):
    return pl.pallas_call(
        merge_kernel,
        out_shape=[struct((128, 512), BF)] * 2,
        in_specs=[VMEM] * 6,
        out_specs=[VMEM] * 2,
        compiler_params=vmem(6),
        name="merge",
    )(*parts)


def mul(left, right):
    return jnp.dot(left.astype(BF), right.astype(BF), preferred_element_type=F32)


def plan_kernel(worker_of, plan):
    z, y, _, _ = position()
    for o in range(4):
        target = z * 4 + ((y + o) & 3)

        def step(b, state):
            count, first, second = state
            hit = worker_of[b] == target
            offset = jnp.where((b & 3) == y, b >> 2, -1)
            first = jnp.where(hit & (count == 0), offset, first)
            second = jnp.where(hit & (count == 1), offset, second)
            return count + hit.astype(jnp.int32), first, second

        none = jnp.int32(-1)
        _, first, second = lax.fori_loop(0, 32, step, (jnp.int32(0), none, none))
        plan[2 * o] = first
        plan[2 * o + 1] = second
        worker = worker_of[target]
        slot = lax.fori_loop(0, target, lambda b, n: n + (worker_of[b] == worker).astype(jnp.int32), jnp.int32(0))
        plan[8 + o] = jnp.where((worker & 3) == y, (worker >> 2) * 2 + slot, -1)
    for n in range(12, 16):
        plan[n] = 0


def make_plan(worker_of):
    return pl.pallas_call(
        plan_kernel,
        out_shape=struct((16,), jnp.int32),
        in_specs=[SMEM],
        out_specs=SMEM,
        name="plan",
    )(worker_of)


def root_kernel(worker_of, left, root, strips, occupied):
    a = 1.5625
    slot = pl.program_id(0)
    z, y, x_place, c = position()
    mine = z * 4 + y
    count = lax.fori_loop(0, 32, lambda b, n: n + (worker_of[b] == mine).astype(jnp.int32), jnp.int32(0))
    matrix = left[0]
    norm = jnp.sqrt(jnp.sum(jnp.sum(matrix * matrix, axis=1, keepdims=True), axis=0, keepdims=True))
    m = matrix / norm
    m2 = mul(m, m)
    p = m2 * 0.0625 - m * 0.625
    u = m * 1.25 - m2 * 0.25
    q = p * (2 * a) + mul(p, p)
    v = u * (a * a) + mul(q, u)
    r = m * -0.3125 - v * 0.25
    s = r * (2 * a) + mul(r, r)
    t = m * a + mul(r, m)
    f = s * (2 * a * a) + mul(s, s)
    w = t * (a * a * a * a) + mul(f, t)
    held = (count > slot).astype(F32)
    occupied[0] = jnp.full((8, 128), held, F32)
    scale = lax.rsqrt(jnp.sqrt(norm)) * held
    row = lax.broadcasted_iota(jnp.int32, (512, 512), 0)
    column = lax.broadcasted_iota(jnp.int32, (512, 512), 1)
    x = jnp.where(row == column, 1.25 * a, 0.0) + r * 1.25 - w * 0.25
    root[0] = x * scale
    strip = c * 64 + x_place * 16
    for n, (i, j) in enumerate(PAIRS):
        rows = pl.ds(pl.multiple_of(i * 128 + strip, 16), 16)
        strips[0, n] = root[0, rows, pl.ds(j * 128, 128)].astype(BF)


def make_roots(worker_of, left):
    return pl.pallas_call(
        root_kernel,
        grid=(2,),
        out_shape=[struct((2, 512, 512), F32), struct((2, 10, 16, 128), BF), struct((2, 8, 128), F32)],
        in_specs=[SMEM, pl.BlockSpec((1, 512, 512), lambda s: (s, 0, 0))],
        out_specs=[pl.BlockSpec((1, 512, 512), lambda s: (s, 0, 0)), pl.BlockSpec((1, 10, 16, 128), lambda s: (s, 0, 0, 0)), pl.BlockSpec((1, 8, 128), lambda s: (s, 0, 0))],
        compiler_params=vmem(10),
        cost_estimate=pl.CostEstimate(flops=2 * 7 * 2 * 512**3, bytes_accessed=4 << 20, transcendentals=0),
        name="roots",
    )(worker_of, left)


def gram_kernel(mine, theirs, keep, send1, send2, send3, acc):
    _, _, x, c = position()
    for n, (i, j) in enumerate(PAIRS):
        total = 0.0
        for part in (mine, theirs):
            total = total + lax.dot_general(
                part[:, pl.ds(i * 128, 128)], part[:, pl.ds(j * 128, 128)], TOKENS_FIRST, preferred_element_type=F32
            )
        acc[n] = total * (1.0 / KV)
    for o, out in enumerate((keep, send1, send2, send3)):
        row = pl.multiple_of(c * 64 + ((x + o) & 3) * 16, 16)
        out[...] = acc[:, pl.ds(row, 16), :].astype(out.dtype)


def grams(mine, theirs):
    return pl.pallas_call(
        gram_kernel,
        out_shape=[struct((10, 16, 128), F32)] + [struct((10, 16, 128), BF)] * 3,
        in_specs=[VMEM, VMEM],
        out_specs=[VMEM] * 4,
        scratch_shapes=[pltpu.VMEM((10, 128, 128), F32)],
        compiler_params=vmem(8),
        name="grams",
    )(mine, theirs)


def choose_kernel(plan, roots, column, *outs):
    for o in range(4):
        for s in range(2):
            index = plan[2 * o + s]
            item = column[jnp.maximum(index, 0)]
            outs[o][s] = jnp.where(index >= 0, item, jnp.zeros_like(item))
        index = plan[8 + o]
        item = roots[jnp.maximum(index, 0)]
        outs[o][2] = jnp.where(index >= 0, item, jnp.zeros_like(item))


def choose(plan, roots, column):
    return pl.pallas_call(
        choose_kernel,
        out_shape=[struct((3, 10, 16, 128), BF)] * 4,
        in_specs=[SMEM, VMEM, VMEM],
        out_specs=[VMEM] * 4,
        compiler_params=vmem(8),
        name="choose",
    )(plan, roots, column)


def finish_kernel(left, occupied, grad, *refs):
    mine, theirs, (stats, update, whole, root) = refs[:4], refs[4:8], refs[8:]
    slot = pl.program_id(0)
    _, _, x, c = position()

    @pl.when(slot == 0)
    def _():
        for side, part in ((c, mine), (1 - c, theirs)):
            for o in range(4):
                row = pl.multiple_of(side * 64 + ((x - o) & 3) * 16, 16)
                whole[:, :, pl.ds(row, 16), :] = part[o][...]

    held = occupied[0, pl.ds(0, 1), :]
    for n, (i, j) in enumerate(PAIRS):
        block = whole[slot, n].astype(F32)
        above = (0, pl.ds(i * 128, 128), pl.ds(j * 128, 128))
        stats[above] = (left[above] + block) * held
        if i != j:
            below = (0, pl.ds(j * 128, 128), pl.ds(i * 128, 128))
            stats[below] = (left[below] + block.T) * held

    @pl.when(slot == 1)
    def _():
        for n, (i, j) in enumerate(PAIRS):
            block = whole[2, n]
            root[pl.ds(i * 128, 128), pl.ds(j * 128, 128)] = block
            if i != j:
                root[pl.ds(j * 128, 128), pl.ds(i * 128, 128)] = block.astype(F32).T.astype(BF)
        update[...] = lax.dot_general(
            root[...], grad[...], (((1,), (1,)), ((), ())), preferred_element_type=F32
        ).astype(BF)


def finish(left, occupied, grad, mine, theirs):
    by_slot = pl.BlockSpec((1, 512, 512), lambda s: (s, 0, 0))
    piece = pl.BlockSpec((3, 10, 16, 128), lambda s: (0, 0, 0, 0))
    return pl.pallas_call(
        finish_kernel,
        grid=(2,),
        out_shape=[struct((2, 512, 512), F32), struct((512, 128), BF)],
        in_specs=[by_slot, pl.BlockSpec((1, 8, 128), lambda s: (s, 0, 0)), pl.BlockSpec((128, 512), lambda s: (0, 0))]
        + [piece] * 8,
        out_specs=[by_slot, pl.BlockSpec((512, 128), lambda s: (0, 0))],
        scratch_shapes=[pltpu.VMEM((3, 10, 128, 128), BF), pltpu.VMEM((512, 512), BF)],
        compiler_params=vmem(10),
        name="finish",
    )(left, occupied, grad, *mine, *theirs)


def local(activations, cotangents, worker_of, left_stats):
    left = left_stats[0]

    sent = pack(activations, cotangents)
    arrived = [shift(p, "y", NY, o + 1) for o, p in enumerate(sent)]
    later, _ = lax.optimization_barrier((left, sent))
    roots, strips, occupied = make_roots(worker_of, later)
    plan = make_plan(worker_of)
    root_strips = lax.all_to_all(jnp.broadcast_to(strips[None], (8, 2, 10, 16, 128)), "z", 0, 0, tiled=True)
    later, _ = lax.optimization_barrier((activations, plan))
    own = keep_own(later)
    last, strips, plan, own = lax.optimization_barrier((arrived[2], strips, plan, own))
    arrived = arrived[:2] + [last]
    swapped = [shift(p, "c", NC, 1) for p in arrived]
    acc, crossed = first_products(own, cotangents, arrived)
    kept, two, six, up, down, half0, half1 = second_products(acc, crossed, swapped)
    up, down = shift(up, "z", NZ, 1), shift(down, "z", NZ, 7)
    ahead, back = merge(two, six, up, down, shift(half0, "z", NZ, 2), shift(half1, "z", NZ, 6))
    kept, root_strips = lax.optimization_barrier((kept, root_strips))
    total = kept + up[0].astype(F32) + down[0].astype(F32)
    total = total + shift(ahead, "z", NZ, 2).astype(F32) + shift(back, "z", NZ, 6).astype(F32)
    grad = total.astype(BF)

    theirs = shift(grad, "c", NC, 1)
    strip, *sends = grams(grad, theirs)
    for o, send in enumerate(sends):
        strip = strip + shift(send, "x", NX, o + 1).astype(F32)
    strip = strip.astype(BF)
    column = lax.all_to_all(jnp.broadcast_to(strip[None], (8, 10, 16, 128)), "z", 0, 0, tiled=True)
    routed = choose(plan, root_strips.reshape(16, 10, 16, 128), column)
    arrived = routed[0]
    for o in (1, 2, 3):
        arrived = arrived + shift(routed[o], "y", NY, o)
    by_x = [arrived] + [shift(arrived, "x", NX, o) for o in (1, 2, 3)]
    by_c = [shift(piece, "c", NC, 1) for piece in by_x]
    new_stats, update = finish(left, occupied, grad, by_x, by_c)
    return new_stats[None], roots[None], update[None]


def solution(mesh):
    fine = Mesh(mesh.devices.reshape(NZ, NY, NX, NC), ("z", "y", "x", "c"))
    dp, mp = ("z", "y"), ("x", "c")
    return jax.shard_map(
        local,
        mesh=fine,
        in_specs=(P(dp, None), P(None, dp, mp), P(), P(dp, None, None, None)),
        out_specs=(P(dp, None, None, None), P(dp, None, None, None), P(dp, None, mp)),
        check_vma=False,
    )
```

```python
import functools

import jax
import jax.numpy as jnp
from jax import lax
from jax.experimental import pallas as pl
from jax.experimental.pallas import tpu as pltpu
from jax.sharding import Mesh, PartitionSpec as P

KV = 1024
NZ, NY, NX, NC = 8, 4, 4, 2
BF = jnp.bfloat16
F32 = jnp.float32
PAIRS = [(i, j) for i in range(4) for j in range(i, 4)]
SMEM = pl.BlockSpec(memory_space=pltpu.SMEM)
VMEM = pl.BlockSpec(memory_space=pltpu.VMEM)
HBM = pl.BlockSpec(memory_space=pltpu.HBM)


def vmem(mebibytes):
    return pltpu.CompilerParams(vmem_limit_bytes=mebibytes * 1024 * 1024)


TOKENS_FIRST = (((0,), (0,)), ((), ()))


def shift(x, axis, size, offset):
    return lax.ppermute(x, axis, [(i, (i + offset) % size) for i in range(size)])


def position():
    return [lax.axis_index(axis) for axis in ("z", "y", "x", "c")]


def struct(shape, dtype):
    return jax.ShapeDtypeStruct(shape, dtype)


def feature_block(place, k, offset):
    return ((place[0] + k) & 3) * 4 + ((place[1] + offset) & 3)


def pack_kernel(act, cot, *refs):
    outs, sems = refs[:3], refs[3]
    place = position()
    half = pl.ds(pl.multiple_of(place[3] * 128, 128), 128)
    copies = []
    for o in (1, 2, 3):
        out = outs[o - 1]
        for k in range(4):
            column = pl.multiple_of(feature_block(place, k, o) * 512, 512)
            copies.append((act.at[half, pl.ds(column, 512)], out.at[:, pl.ds(k * 512, 512)]))
        for h in range(2):
            for m in range(2):
                lane = 2048 + h * 256 + m * 128
                copies.append((cot.at[m, pl.ds(h * 128, 128), :], out.at[:, pl.ds(lane, 128)]))
    started = []
    for n, (source, target) in enumerate(copies):
        copy = pltpu.make_async_copy(source, target, sems.at[n])
        copy.start()
        started.append(copy)
    for copy in started:
        copy.wait()


def pack(act, cot):
    return pl.pallas_call(
        pack_kernel,
        out_shape=[struct((128, 2560), BF)] * 3,
        in_specs=[HBM, HBM],
        out_specs=[VMEM] * 3,
        scratch_shapes=[pltpu.SemaphoreType.DMA((24,))],
        compiler_params=vmem(60),
        name="pack",
    )(act, cot)


def own_kernel(act, own, sems):
    place = position()
    copies = []
    for k in range(4):
        column = pl.multiple_of(feature_block(place, k, 0) * 512, 512)
        copies.append(pltpu.make_async_copy(act.at[:, pl.ds(column, 512)], own.at[:, pl.ds(k * 512, 512)], sems.at[k]))
        copies[k].start()
    for copy in copies:
        copy.wait()


def keep_own(act):
    return pl.pallas_call(
        own_kernel,
        out_shape=struct((256, 2048), BF),
        in_specs=[HBM],
        out_specs=VMEM,
        scratch_shapes=[pltpu.SemaphoreType.DMA((4,))],
        compiler_params=vmem(8),
        name="own",
    )(act)


def first_kernel(own, cot, *refs):
    pieces, acc, crossed, lhs = refs[:3], refs[3], refs[4], refs[5]
    c = position()[3]
    straight = pl.multiple_of(c * 256, 256)
    other = pl.multiple_of(256 - c * 256, 256)
    for m in range(2):
        lhs[pl.ds(m * 128, 128), pl.ds(0, 256)] = cot[m].T
    for o in range(3):
        lhs[:, pl.ds(256 + o * 128, 128)] = pieces[o][:, pl.ds(2048 + straight, 256)].T
        crossed[:, pl.ds(o * 128, 128)] = pieces[o][:, pl.ds(2048 + other, 256)].T
    for n in range(8):
        column = pl.ds(n * 256, 256)
        total = jnp.dot(lhs[:, pl.ds(0, 256)], own[:, column], preferred_element_type=F32)
        for o in range(3):
            left = lhs[:, pl.ds(256 + o * 128, 128)]
            total = total + jnp.dot(left, pieces[o][:, column], preferred_element_type=F32)
        acc[:, column] = total


def first_products(own, cot, pieces):
    return pl.pallas_call(
        first_kernel,
        out_shape=[struct((256, 2048), F32), struct((256, 384), BF)],
        in_specs=[VMEM] * 5,
        out_specs=[VMEM] * 2,
        scratch_shapes=[pltpu.VMEM((256, 640), BF)],
        compiler_params=vmem(10),
        cost_estimate=pl.CostEstimate(flops=2048 * 256 * 1024, bytes_accessed=4 << 20, transcendentals=0),
        name="first",
    )(own, cot, *pieces)


def second_kernel(acc, crossed, *refs):
    swaps, (kept, two, six, up, down, half0, half1, total) = refs[:3], refs[3:]
    z = position()[0]
    for k in range(4):
        m = ((z + k) & 7) >> 2
        for half in range(2):
            column = pl.ds(k * 512 + half * 256, 256)
            value = acc[:, column]
            for o in range(3):
                value = value + jnp.dot(
                    crossed[:, pl.ds(o * 128, 128)], swaps[o][:, column], preferred_element_type=F32
                )
            total[...] = value
            lanes = pl.ds(half * 256, 256)
            near = total[pl.ds(pl.multiple_of(m * 128, 128), 128), :]
            far = total[pl.ds(pl.multiple_of(128 - m * 128, 128), 128), :]
            if k == 0:
                kept[:, lanes] = near
                half0[:, lanes] = far[:64].astype(BF)
                half1[:, lanes] = far[64:].astype(BF)
            elif k == 2:
                two[:, lanes] = near
                six[:, lanes] = far
            else:
                up[k // 2, :, lanes] = near.astype(BF)
                down[1 - k // 2, :, lanes] = far.astype(BF)


def second_products(acc, crossed, swaps):
    return pl.pallas_call(
        second_kernel,
        out_shape=[struct((128, 512), F32)] * 3 + [struct((2, 128, 512), BF)] * 2 + [struct((64, 512), BF)] * 2,
        in_specs=[VMEM] * 5,
        out_specs=[VMEM] * 7,
        scratch_shapes=[pltpu.VMEM((256, 256), F32)],
        compiler_params=vmem(10),
        cost_estimate=pl.CostEstimate(flops=2048 * 256 * 1024, bytes_accessed=4 << 20, transcendentals=0),
        name="second",
    )(acc, crossed, *swaps)


def merge_kernel(two, six, up, down, low, high, ahead, back):
    ahead[pl.ds(0, 64), :] = (two[pl.ds(0, 64), :] + up[1, pl.ds(0, 64), :].astype(F32) + low[...].astype(F32)).astype(BF)
    ahead[pl.ds(64, 64), :] = (two[pl.ds(64, 64), :] + up[1, pl.ds(64, 64), :].astype(F32)).astype(BF)
    back[pl.ds(0, 64), :] = (six[pl.ds(0, 64), :] + down[1, pl.ds(0, 64), :].astype(F32)).astype(BF)
    back[pl.ds(64, 64), :] = (six[pl.ds(64, 64), :] + down[1, pl.ds(64, 64), :].astype(F32) + high[...].astype(F32)).astype(BF)


def merge(*parts):
    return pl.pallas_call(
        merge_kernel,
        out_shape=[struct((128, 512), BF)] * 2,
        in_specs=[VMEM] * 6,
        out_specs=[VMEM] * 2,
        compiler_params=vmem(6),
        name="merge",
    )(*parts)


def mul(left, right):
    return jnp.dot(left.astype(BF), right.astype(BF), preferred_element_type=F32)


def plan_kernel(worker_of, plan):
    z, y, _, _ = position()
    for o in range(4):
        target = z * 4 + ((y + o) & 3)

        def step(b, state):
            count, first, second = state
            hit = worker_of[b] == target
            offset = jnp.where((b & 3) == y, b >> 2, -1)
            first = jnp.where(hit & (count == 0), offset, first)
            second = jnp.where(hit & (count == 1), offset, second)
            return count + hit.astype(jnp.int32), first, second

        none = jnp.int32(-1)
        _, first, second = lax.fori_loop(0, 32, step, (jnp.int32(0), none, none))
        plan[2 * o] = first
        plan[2 * o + 1] = second
        worker = worker_of[target]
        slot = lax.fori_loop(0, target, lambda b, n: n + (worker_of[b] == worker).astype(jnp.int32), jnp.int32(0))
        plan[8 + o] = jnp.where((worker & 3) == y, (worker >> 2) * 2 + slot, -1)
    for n in range(12, 16):
        plan[n] = 0


def make_plan(worker_of):
    return pl.pallas_call(
        plan_kernel,
        out_shape=struct((16,), jnp.int32),
        in_specs=[SMEM],
        out_specs=SMEM,
        name="plan",
    )(worker_of)


def root_kernel(worker_of, left, root, strips, occupied):
    a = 1.5625
    slot = pl.program_id(0)
    z, y, x_place, c = position()
    mine = z * 4 + y
    count = lax.fori_loop(0, 32, lambda b, n: n + (worker_of[b] == mine).astype(jnp.int32), jnp.int32(0))
    matrix = left[0]
    norm = jnp.sqrt(jnp.sum(jnp.sum(matrix * matrix, axis=1, keepdims=True), axis=0, keepdims=True))
    m = matrix / norm
    m2 = mul(m, m)
    p = m2 * 0.0625 - m * 0.625
    u = m * 1.25 - m2 * 0.25
    q = p * (2 * a) + mul(p, p)
    v = u * (a * a) + mul(q, u)
    r = m * -0.3125 - v * 0.25
    s = r * (2 * a) + mul(r, r)
    t = m * a + mul(r, m)
    f = s * (2 * a * a) + mul(s, s)
    w = t * (a * a * a * a) + mul(f, t)
    held = (count > slot).astype(F32)
    occupied[0] = jnp.full((8, 128), held, F32)
    scale = lax.rsqrt(jnp.sqrt(norm)) * held
    row = lax.broadcasted_iota(jnp.int32, (512, 512), 0)
    column = lax.broadcasted_iota(jnp.int32, (512, 512), 1)
    x = jnp.where(row == column, 1.25 * a, 0.0) + r * 1.25 - w * 0.25
    root[0] = x * scale
    strip = c * 64 + x_place * 16
    for n, (i, j) in enumerate(PAIRS):
        rows = pl.ds(pl.multiple_of(i * 128 + strip, 16), 16)
        strips[0, n] = root[0, rows, pl.ds(j * 128, 128)].astype(BF)


def make_roots(worker_of, left):
    return pl.pallas_call(
        root_kernel,
        grid=(2,),
        out_shape=[struct((2, 512, 512), F32), struct((2, 10, 16, 128), BF), struct((2, 8, 128), F32)],
        in_specs=[SMEM, pl.BlockSpec((1, 512, 512), lambda s: (s, 0, 0))],
        out_specs=[pl.BlockSpec((1, 512, 512), lambda s: (s, 0, 0)), pl.BlockSpec((1, 10, 16, 128), lambda s: (s, 0, 0, 0)), pl.BlockSpec((1, 8, 128), lambda s: (s, 0, 0))],
        compiler_params=vmem(10),
        cost_estimate=pl.CostEstimate(flops=2 * 7 * 2 * 512**3, bytes_accessed=4 << 20, transcendentals=0),
        name="roots",
    )(worker_of, left)


def gram_kernel(mine, theirs, keep, send1, send2, send3, acc):
    _, _, x, c = position()
    for n, (i, j) in enumerate(PAIRS):
        total = 0.0
        for part in (mine, theirs):
            total = total + lax.dot_general(
                part[:, pl.ds(i * 128, 128)], part[:, pl.ds(j * 128, 128)], TOKENS_FIRST, preferred_element_type=F32
            )
        acc[n] = total * (1.0 / KV)
    for o, out in enumerate((keep, send1, send2, send3)):
        row = pl.multiple_of(c * 64 + ((x + o) & 3) * 16, 16)
        out[...] = acc[:, pl.ds(row, 16), :].astype(out.dtype)


def grams(mine, theirs):
    return pl.pallas_call(
        gram_kernel,
        out_shape=[struct((10, 16, 128), F32)] + [struct((10, 16, 128), BF)] * 3,
        in_specs=[VMEM, VMEM],
        out_specs=[VMEM] * 4,
        scratch_shapes=[pltpu.VMEM((10, 128, 128), F32)],
        compiler_params=vmem(8),
        name="grams",
    )(mine, theirs)


def choose_kernel(plan, roots, column, *outs):
    for o in range(4):
        for s in range(2):
            index = plan[2 * o + s]
            item = column[jnp.maximum(index, 0)]
            outs[o][s] = jnp.where(index >= 0, item, jnp.zeros_like(item))
        index = plan[8 + o]
        item = roots[jnp.maximum(index, 0)]
        outs[o][2] = jnp.where(index >= 0, item, jnp.zeros_like(item))


def choose(plan, roots, column):
    return pl.pallas_call(
        choose_kernel,
        out_shape=[struct((3, 10, 16, 128), BF)] * 4,
        in_specs=[SMEM, VMEM, VMEM],
        out_specs=[VMEM] * 4,
        compiler_params=vmem(8),
        name="choose",
    )(plan, roots, column)


def finish_kernel(left, occupied, grad, *refs):
    mine, theirs, (stats, update, whole, root) = refs[:4], refs[4:8], refs[8:]
    slot = pl.program_id(0)
    _, _, x, c = position()

    @pl.when(slot == 0)
    def _():
        for side, part in ((c, mine), (1 - c, theirs)):
            for o in range(4):
                row = pl.multiple_of(side * 64 + ((x - o) & 3) * 16, 16)
                whole[:, :, pl.ds(row, 16), :] = part[o][...]

    held = occupied[0, pl.ds(0, 1), :]
    for n, (i, j) in enumerate(PAIRS):
        block = whole[slot, n].astype(F32)
        above = (0, pl.ds(i * 128, 128), pl.ds(j * 128, 128))
        stats[above] = (left[above] + block) * held
        if i != j:
            below = (0, pl.ds(j * 128, 128), pl.ds(i * 128, 128))
            stats[below] = (left[below] + block.T) * held

    @pl.when(slot == 1)
    def _():
        for n, (i, j) in enumerate(PAIRS):
            block = whole[2, n]
            root[pl.ds(i * 128, 128), pl.ds(j * 128, 128)] = block
            if i != j:
                root[pl.ds(j * 128, 128), pl.ds(i * 128, 128)] = block.astype(F32).T.astype(BF)
        update[...] = lax.dot_general(
            root[...], grad[...], (((1,), (1,)), ((), ())), preferred_element_type=F32
        ).astype(BF)


def finish(left, occupied, grad, mine, theirs):
    by_slot = pl.BlockSpec((1, 512, 512), lambda s: (s, 0, 0))
    piece = pl.BlockSpec((3, 10, 16, 128), lambda s: (0, 0, 0, 0))
    return pl.pallas_call(
        finish_kernel,
        grid=(2,),
        out_shape=[struct((2, 512, 512), F32), struct((512, 128), BF)],
        in_specs=[by_slot, pl.BlockSpec((1, 8, 128), lambda s: (s, 0, 0)), pl.BlockSpec((128, 512), lambda s: (0, 0))]
        + [piece] * 8,
        out_specs=[by_slot, pl.BlockSpec((512, 128), lambda s: (0, 0))],
        scratch_shapes=[pltpu.VMEM((3, 10, 128, 128), BF), pltpu.VMEM((512, 512), BF)],
        compiler_params=vmem(10),
        name="finish",
    )(left, occupied, grad, *mine, *theirs)


def local(activations, cotangents, worker_of, left_stats):
    left = left_stats[0]

    sent = pack(activations, cotangents)
    arrived = [shift(p, "y", NY, o + 1) for o, p in enumerate(sent)]
    later, _ = lax.optimization_barrier((left, sent))
    roots, strips, occupied = make_roots(worker_of, later)
    plan = make_plan(worker_of)
    root_strips = lax.all_to_all(jnp.broadcast_to(strips[None], (8, 2, 10, 16, 128)), "z", 0, 0, tiled=True)
    later, _ = lax.optimization_barrier((activations, plan))
    own = keep_own(later)
    arrived, strips, plan, own = lax.optimization_barrier((arrived, strips, plan, own))
    swapped = [shift(p, "c", NC, 1) for p in arrived]
    acc, crossed = first_products(own, cotangents, arrived)
    kept, two, six, up, down, half0, half1 = second_products(acc, crossed, swapped)
    up, down = shift(up, "z", NZ, 1), shift(down, "z", NZ, 7)
    ahead, back = merge(two, six, up, down, shift(half0, "z", NZ, 2), shift(half1, "z", NZ, 6))
    total = kept + up[0].astype(F32) + down[0].astype(F32)
    total = total + shift(ahead, "z", NZ, 2).astype(F32) + shift(back, "z", NZ, 6).astype(F32)
    grad = total.astype(BF)

    theirs = shift(grad, "c", NC, 1)
    strip, *sends = grams(grad, theirs)
    for o, send in enumerate(sends):
        strip = strip + shift(send, "x", NX, o + 1).astype(F32)
    strip, root_strips = lax.optimization_barrier((strip.astype(BF), root_strips))
    column = lax.all_to_all(jnp.broadcast_to(strip[None], (8, 10, 16, 128)), "z", 0, 0, tiled=True)
    routed = choose(plan, root_strips.reshape(16, 10, 16, 128), column)
    arrived = routed[0]
    for o in (1, 2, 3):
        arrived = arrived + shift(routed[o], "y", NY, o)
    by_x = [arrived] + [shift(arrived, "x", NX, o) for o in (1, 2, 3)]
    by_c = [shift(piece, "c", NC, 1) for piece in by_x]
    new_stats, update = finish(left, occupied, grad, by_x, by_c)
    return new_stats[None], roots[None], update[None]


def solution(mesh):
    fine = Mesh(mesh.devices.reshape(NZ, NY, NX, NC), ("z", "y", "x", "c"))
    dp, mp = ("z", "y"), ("x", "c")
    return jax.shard_map(
        local,
        mesh=fine,
        in_specs=(P(dp, None), P(None, dp, mp), P(), P(dp, None, None, None)),
        out_specs=(P(dp, None, None, None), P(dp, None, None, None), P(dp, None, mp)),
        check_vma=False,
    )
```
